256 devices in a mesh: ctx: 32 (over y, z), heads: 8 (over x, core).
Axes of the slice: x: 4, y: 4, z: 8, core: 2. Of those that a mesh axis runs over, the one named last changes fastest.
Arguments:
- mixer_input: bfloat16 [32768, 6144], P('ctx', 'heads'), parts along dimension 1, may hold values from -6 to 6
- conv_weight: float32 [4, 6144], P(None, 'heads'), parts along dimension 1, may hold values from -3 to 3
- log_decay: float32 [64, 32768], P('heads', 'ctx'), parts along dimension 0, may hold values from -1 to 0
- level_weight: float32 [7, 64, 32768], P(None, 'heads', 'ctx'), parts along dimension 1, may hold values from 0.2 to 2
- norm_gain: float32 [4096], P('heads'), parts along dimension 0, may hold values from 0.5 to 1.5
Outputs:
- normed_output: bfloat16 [32768, 4096], P('ctx', 'heads'), parts along dimension 1
The draws below stay inside these ranges and needn't reach their ends.
There are 8 independent parts, one for each index of `heads`. The reference program is written for one: setup_inputs(seed, part) draws one part's arguments, and reference() takes and returns one part's arrays. A program takes and returns all parts, laid end to end along the dimension named above; each array names one. Nothing has to cross between parts.
All inputs are finite; a program needn't handle non-finite values.
Results may differ from the reference program's by a relative error of at most 0.0075.
Values may be sent and summed in bfloat16 or wider, within the bound.
A program may use at most 128 MiB of HBM per device.

```python
import math
import jax
import jax.numpy as jnp
from jax import lax

HEADS_PART = 8
HEAD_DIM = 64
STATE = 128
CONV_K = 4
STRETCH = 256
LEVELS = 7
TOK_DEV = 1024
SEQUENCE_TOKENS = 32768
WIDTH_G = 512
CONV_W = 768
N_CTX = 32


def draw_log_decay(key, part):
    random_subkeys = jax.random.split(key, 6)
    ranking = jax.random.permutation(random_subkeys[0], HEADS_PART)
    slow_count = HEADS_PART // 2
    is_slow = (ranking < slow_count)[:, None]
    slow_rate = jax.random.uniform(random_subkeys[1], (HEADS_PART, 1), jnp.float32, 0.1, 0.8) / SEQUENCE_TOKENS
    fast_rate = jax.random.uniform(random_subkeys[2], (HEADS_PART, 1), jnp.float32, 1.0 / 50.0, 1.0 / 30.0)
    jitter = jax.random.uniform(random_subkeys[3], (HEADS_PART, SEQUENCE_TOKENS), jnp.float32, 0.5, 1.5)
    token_wise = jnp.where(is_slow, slow_rate, fast_rate) * jitter
    spike_position = jax.random.randint(random_subkeys[4], (2,), 0, SEQUENCE_TOKENS)
    spike_penalty = jnp.log(jax.random.uniform(random_subkeys[5], (2, 1), jnp.float32, 0.5, 0.8))
    spike_landed = jnp.arange(SEQUENCE_TOKENS)[None, :] == spike_position[:, None]
    spike_events = jnp.sum(jnp.where(spike_landed, spike_penalty, 0.0), axis=0)
    return -token_wise + spike_events[None, :]


def block_scale(rng, shape, cuts, low, high):
    def one(axis_at, shards_of):
        steps = jax.random.uniform(jax.random.fold_in(jax.random.fold_in(rng, 6), axis_at), (shards_of,), jnp.float32, low / len(cuts), high / len(cuts))
        return jnp.repeat(jnp.exp(steps), shape[axis_at] // shards_of).reshape((-1,) + (1,) * (len(shape) - axis_at - 1))

    factor_of = one(*cuts[0])
    for cut in cuts[1:]:
        factor_of = factor_of * one(*cut)
    return factor_of


def normal_values(rng, dims, width, reach, cuts=(), kind=jnp.bfloat16):
    result = jax.random.normal(rng, dims, jnp.float32) * width
    if len(cuts) > 0:
        result = block_scale(rng, dims, cuts, -0.22, 0.18) * result
    return jnp.clip(result, min=-reach, max=reach).astype(kind)


def setup_inputs(seed: int = 0, part: int = 0) -> dict:
    keys = jax.random.split(jax.random.key(seed), 6)
    part_splits = jax.random.split(jax.random.fold_in(keys[5], part), 6)
    return {
        "mixer_input": normal_values(part_splits[0], (SEQUENCE_TOKENS, CONV_W), 1.0, 6.0, ((0, 32),)),
        "conv_weight": normal_values(part_splits[1], (CONV_K, CONV_W), CONV_K ** -0.5, 3.0, (), jnp.float32),
        "log_decay": draw_log_decay(jax.random.fold_in(jax.random.fold_in(keys[5], part), 71), part),
        "level_weight": jnp.clip(jnp.exp(math.log(2.0) - 2.3025851 * jax.random.uniform(part_splits[3], (LEVELS, HEADS_PART, SEQUENCE_TOKENS), jnp.float32) ** block_scale(part_splits[3], (LEVELS, HEADS_PART, SEQUENCE_TOKENS), ((2, 32),), -0.2, 0.2)), 0.2, 2.0),
        "norm_gain": jnp.clip(1.0 + 0.1 * jax.random.normal(part_splits[4], (WIDTH_G,), jnp.float32), 0.5, 1.5),
    }


def convolve(mixer_input, rim_rows, conv_weight):
    padded = jnp.concatenate([rim_rows, mixer_input], axis=0)
    row_count = mixer_input.shape[0]
    running = jnp.zeros(mixer_input.shape, jnp.float32)
    for tap_row in range(conv_weight.shape[0]):
        running = running + conv_weight[tap_row] * padded[tap_row:tap_row + row_count]
    return jax.nn.silu(running).astype(jnp.bfloat16)

def shard_terms(activated, log_decay, level_weight):
    row_count = activated.shape[0]
    stretches = row_count // STRETCH
    inputs_all = activated[:, :WIDTH_G].reshape(stretches, STRETCH, HEADS_PART, HEAD_DIM)
    keys_all = activated[:, WIDTH_G:WIDTH_G + STATE].reshape(stretches, STRETCH, STATE)
    query_all = activated[:, WIDTH_G + STATE:].reshape(stretches, STRETCH, STATE)
    rate_all = log_decay.reshape(HEADS_PART, stretches, STRETCH).transpose(1, 0, 2)
    weight_all = level_weight[:2].reshape(2, HEADS_PART, stretches, STRETCH).transpose(2, 0, 1, 3)
    causal = jnp.arange(STRETCH)[:, None] >= jnp.arange(STRETCH)[None, :]

    def one_stretch(pieces):
        stretch_in, stretch_keys, stretch_query, stretch_rate, stretch_weight = pieces
        inner_sum = jnp.cumsum(stretch_rate, axis=1)
        scores = jnp.dot(stretch_query, stretch_keys.T, preferred_element_type=jnp.float32)
        decay_gap = inner_sum[:, :, None] - inner_sum[:, None, :]
        decay_map = jnp.exp(jnp.where(causal[None], decay_gap, -jnp.inf))
        mixing = (stretch_weight[0][:, :, None] * decay_map * scores[None]).astype(jnp.bfloat16)
        own_stretch = jnp.einsum('hqk,khp->qhp', mixing, stretch_in, preferred_element_type=jnp.float32)
        to_end = jnp.exp(inner_sum[:, -1:] - inner_sum)
        scaled = (to_end[:, :, None] * stretch_keys[None]).astype(jnp.bfloat16)
        stretch_state = jnp.einsum('hqn,qhp->nhp', scaled, stretch_in, preferred_element_type=jnp.float32)
        return (own_stretch, stretch_state, inner_sum)
    own_all, state_all, inner_all = lax.map(one_stretch, (inputs_all, keys_all, query_all, rate_all, weight_all))
    totals = inner_all[:, :, -1]

    def carry_step(carried, pieces):
        stretch_state, stretch_total = pieces
        return (jnp.exp(stretch_total)[None, :, None] * carried + stretch_state, carried)
    shard_end, starts = lax.scan(carry_step, jnp.zeros((STATE, HEADS_PART, HEAD_DIM), jnp.float32), (state_all, totals))
    readout = jnp.einsum('cqn,cnhp->cqhp', query_all, starts.astype(jnp.bfloat16), preferred_element_type=jnp.float32)
    inner_rows = inner_all.transpose(0, 2, 1)
    near_scale = weight_all[:, 1].transpose(0, 2, 1) * jnp.exp(inner_rows)
    mixture = own_all + near_scale[..., None] * readout
    offset = jnp.cumsum(totals, axis=0) - totals
    from_start = jnp.exp(offset[:, None, :] + inner_rows).reshape(row_count, HEADS_PART)
    return (mixture.reshape(row_count, WIDTH_G), shard_end.reshape(STATE, WIDTH_G), lax.optimization_barrier(jnp.sum(totals, axis=0)), from_start)

def fenwick_buckets(every_end, every_span, reader, bit_count):
    shards = every_end.shape[0]
    before_all = jnp.cumsum(every_span, axis=0) - every_span
    start_at = lax.dynamic_index_in_dim(before_all, reader, 0, keepdims=False)
    decay_gap = start_at[None, :] - before_all - every_span
    source = jnp.arange(shards, dtype=jnp.int32)
    grouped = every_end.reshape(shards, STATE, HEADS_PART, HEAD_DIM)
    buckets = []
    for level_num in range(bit_count):
        member = (source // 2 ** level_num == reader // 2 ** level_num - 1) & (reader // 2 ** level_num % 2 == 1)
        factor = jnp.exp(jnp.where(member[:, None], decay_gap, -jnp.inf))
        bucket = jnp.einsum('sh,snhp->nhp', factor, grouped, precision=lax.Precision.HIGHEST)
        buckets.append(bucket.reshape(STATE, WIDTH_G))
    return buckets

def read_levels(queries, buckets, level_weight, from_start):
    row_count = queries.shape[0]
    running = jnp.zeros((row_count, HEADS_PART, HEAD_DIM), jnp.float32)
    for level_num, bucket in enumerate(buckets):
        readout = jnp.dot(queries, bucket.astype(jnp.bfloat16), preferred_element_type=jnp.float32)
        running = running + level_weight[2 + level_num].T[:, :, None] * readout.reshape(row_count, HEADS_PART, HEAD_DIM)
    return (running * from_start[:, :, None]).reshape(row_count, WIDTH_G)

def normalize(mixture, norm_gain):
    mean_square = lax.optimization_barrier(jnp.mean(mixture * mixture, axis=1, keepdims=True))
    return (mixture * lax.rsqrt(mean_square + 1e-05) * norm_gain).astype(jnp.bfloat16)

def reference(mixer_input, conv_weight, log_decay, level_weight, norm_gain):
    tap_count = conv_weight.shape[0]
    rim_rows = jnp.zeros((tap_count - 1, mixer_input.shape[1]), mixer_input.dtype)
    activated = convolve(mixer_input, rim_rows, conv_weight)
    shard_act = activated.reshape(N_CTX, TOK_DEV, CONV_W)
    shard_decay = log_decay.reshape(HEADS_PART, N_CTX, TOK_DEV).transpose(1, 0, 2)
    shard_levels = level_weight.reshape(LEVELS, HEADS_PART, N_CTX, TOK_DEV).transpose(2, 0, 1, 3)

    def summarize(pieces):
        outcome = shard_terms(pieces[0], pieces[1], pieces[2])
        return (outcome[1], outcome[2])
    every_end, every_span = lax.map(summarize, (shard_act, shard_decay, shard_levels))
    bit_count = N_CTX.bit_length() - 1
    readers = jnp.arange(N_CTX, dtype=jnp.int32)

    def finish(pieces):
        one_act, decays, levels, reader = pieces
        mixture, shard_end, shard_total, from_start = shard_terms(one_act, decays, levels)
        buckets = fenwick_buckets(every_end, every_span, reader, bit_count)
        mixture = mixture + read_levels(one_act[:, WIDTH_G + STATE:], buckets, levels, from_start)
        return normalize(mixture, norm_gain)
    outputs = lax.map(finish, (shard_act, shard_decay, shard_levels, readers))
    return outputs.reshape(SEQUENCE_TOKENS, WIDTH_G)
```

```python
import functools

import jax
import jax.numpy as jnp
from jax import lax
from jax.experimental import pallas as pl
from jax.experimental.pallas import tpu as pltpu
from jax.sharding import PartitionSpec as P

HEADS = 8
HEAD_DIM = 64
STATE = 128
STRETCH = 256
WIDTH = 512
TOKENS = 1024
PIECES = TOKENS // STRETCH
SHARDS = 32
BITS = 5
HALF = 128
ROWS = WIDTH // SHARDS
LOG2E = 1.4426950408889634

NT = (((1,), (1,)), ((), ()))
F32 = jnp.float32
BF16 = jnp.bfloat16


def popcount(r):
    count = r % 2
    for k in range(1, BITS):
        count = count + (r // 2**k) % 2
    return count


def activate(window, conv_ref, cols):
    total = conv_ref[3:4, cols] * window[16:144]
    for j in range(3):
        total = total + conv_ref[j : j + 1, cols] * window[13 + j : 141 + j]
    half = 0.5 * total
    return (half + half * jnp.tanh(half)).astype(BF16)


def kernel(
    x_ref, conv_ref, rate_ref, level_ref, gain_ref, out_ref,
    halo, xt, keys, qt, inner, column, state, low, mixed, gain_col, slot_weight,
    send1, recv1, own_span, spans, stage, recv3,
    halo_sem, p1_send, p1_recv, span_send, span_recv, p3_send, p3_recv,
):
    me = lax.axis_index("ctx")
    bits = popcount(me)

    barrier = pltpu.get_barrier_semaphore()
    recv3[...] = jnp.zeros_like(recv3)

    def greet(d, _):
        other = lax.rem(me + d, SHARDS)
        pl.semaphore_signal(barrier, inc=1, device_id={"ctx": other})
        return 0

    lax.fori_loop(1, SHARDS, greet, 0)

    rows = lax.broadcasted_iota(jnp.int32, (STRETCH, STRETCH), 0)
    cols = lax.broadcasted_iota(jnp.int32, (STRETCH, STRETCH), 1)
    lower = jnp.where(rows >= cols, 1.0, 0.0).astype(F32)
    span = jnp.zeros((HEADS, HALF), F32)
    for c in range(PIECES):
        rate = rate_ref[:, c * STRETCH : (c + 1) * STRETCH] * LOG2E
        inner[c] = lax.dot_general(
            rate, lower, NT, precision=lax.Precision.HIGHEST, preferred_element_type=F32
        )
        column[c] = lax.dot_general(
            lower, rate, NT, precision=lax.Precision.HIGHEST, preferred_element_type=F32
        )
        span = span + jnp.broadcast_to(inner[c, :, STRETCH - 1 :], (HEADS, HALF))
    own_span[...] = span

    diag = (rows == cols)[:HALF, :HALF]
    for g in range(WIDTH // HALF):
        row = jnp.broadcast_to(gain_ref[:, g * HALF : (g + 1) * HALF], (HALF, HALF))
        gain_col[g * HALF : (g + 1) * HALF] = jnp.sum(
            jnp.where(diag, row, 0.0), axis=1, keepdims=True
        )

    def place(b, group, act):
        c, half = b // 2, b % 2
        if group < 4:
            xt[c, half, group * HALF : (group + 1) * HALF] = act.T
        elif group == 4:
            keys[c, pl.ds(pl.multiple_of(half * HALF, HALF), HALF)] = act
        else:
            qt[c, half] = act.T

    def block(i, _):
        b = TOKENS // HALF - 1 - i
        start = pl.multiple_of(b * HALF - 16, 16)
        for group in range(6):
            chans = slice(group * HALF, (group + 1) * HALF)
            window = x_ref[pl.ds(start, HALF + 16), chans].astype(F32)
            place(b, group, activate(window, conv_ref, chans))
        return 0

    lax.fori_loop(0, TOKENS // HALF - 1, block, 0)

    pl.semaphore_wait(barrier, SHARDS - 1)
    to_next = pltpu.make_async_remote_copy(
        src_ref=x_ref.at[pl.ds(TOKENS - 16, 16)], dst_ref=halo,
        send_sem=halo_sem.at[0], recv_sem=halo_sem.at[1],
        device_id={"ctx": lax.rem(me + 1, SHARDS)},
    )

    @pl.when(me < SHARDS - 1)
    def _():
        to_next.start()

    def stretch_state(c):
        to_end = jnp.exp2(inner[c, :, STRETCH - 1 :] - inner[c])
        parts = []
        for h in range(HEADS):
            x_h = jnp.concatenate(
                [xt[c, 0, h * HEAD_DIM : (h + 1) * HEAD_DIM], xt[c, 1, h * HEAD_DIM : (h + 1) * HEAD_DIM]],
                axis=1,
            )
            parts.append((x_h.astype(F32) * to_end[h : h + 1]).astype(BF16))
        state[c] = jnp.dot(
            jnp.concatenate(parts, axis=0), keys[c], preferred_element_type=F32
        )

    def late(i, _):
        stretch_state(PIECES - 1 - i)
        return 0

    lax.fori_loop(0, PIECES - 1, late, 0)

    @pl.when(me == 0)
    def _():
        halo[...] = jnp.zeros_like(halo)

    @pl.when(me > 0)
    def _():
        to_next.wait_recv()

    for group in range(6):
        chans = slice(group * HALF, (group + 1) * HALF)
        window = jnp.concatenate([halo[:, chans], x_ref[:HALF, chans]], axis=0).astype(F32)
        place(0, group, activate(window, conv_ref, chans))
    stretch_state(0)

    for h in range(HEADS):
        at = slice(h * HEAD_DIM, (h + 1) * HEAD_DIM)
        carried = state[0, at]
        for c in range(1, PIECES):
            low[c - 1, at] = carried.astype(BF16)
            fall = jnp.exp2(
                jnp.broadcast_to(inner[c, h : h + 1, STRETCH - 1 :], (1, STATE))
            )
            carried = fall * carried + state[c, at]
        send1[4 * h : 4 * (h + 1)] = carried.astype(BF16).reshape(4, ROWS, STATE)

    def spread(d, _):
        other = lax.rem(me + d, SHARDS)
        pltpu.make_async_remote_copy(
            src_ref=send1.at[other], dst_ref=recv1.at[me],
            send_sem=p1_send, recv_sem=p1_recv, device_id={"ctx": other},
        ).start()
        return 0

    lax.fori_loop(1, SHARDS, spread, 0)

    def spread_span(d, _):
        other = lax.rem(me + d, SHARDS)
        pltpu.make_async_remote_copy(
            src_ref=own_span, dst_ref=spans.at[me],
            send_sem=span_send, recv_sem=span_recv, device_id={"ctx": other},
        ).start()
        return 0

    lax.fori_loop(1, SHARDS, spread_span, 0)
    recv1[me] = send1[me]
    spans[me] = own_span[...]

    causal = (rows <= cols)[:HALF, :HALF]

    def near_own(c, before):
        q = [qt[c, 0], qt[c, 1]]
        k = keys[c]
        for half in range(2):
            width = HALF * (half + 1)
            score = jnp.dot(k[:width], q[half], preferred_element_type=F32)
            at_t = pl.ds(pl.multiple_of(c * STRETCH, STRETCH) + half * HALF, HALF)
            row_all = inner[c, :, half * HALF : (half + 1) * HALF]
            own_scale = level_ref[0, :, at_t]
            near_scale = level_ref[1, :, at_t] * jnp.exp2(row_all)
            if before:
                readout = jnp.dot(low[c - 1], q[half], preferred_element_type=F32)
            for h in range(HEADS):
                at = slice(h * HEAD_DIM, (h + 1) * HEAD_DIM)
                gap = row_all[h : h + 1] - column[c, :width, h : h + 1]
                blocks = []
                if half == 1:
                    blocks.append((jnp.exp2(gap[:HALF]) * score[:HALF]).astype(BF16))
                last = jnp.where(causal, gap[width - HALF :], -jnp.inf)
                blocks.append((jnp.exp2(last) * score[width - HALF :]).astype(BF16))
                own = jnp.dot(xt[c, half, at], blocks[-1], preferred_element_type=F32)
                if half == 1:
                    own = own + jnp.dot(xt[c, 0, at], blocks[0], preferred_element_type=F32)
                own = own * own_scale[h : h + 1]
                if before:
                    own = own + readout[at] * near_scale[h : h + 1]
                mixed[c, half, at] = own

    near_own(0, False)

    def rest(c, _):
        near_own(c, True)
        return 0

    lax.fori_loop(1, PIECES, rest, 0)

    pltpu.make_async_remote_copy(
        src_ref=send1.at[pl.ds(0, SHARDS - 1)], dst_ref=recv1.at[pl.ds(0, SHARDS - 1)],
        send_sem=p1_send, recv_sem=p1_recv, device_id={"ctx": lax.rem(me + 1, SHARDS)},
    ).wait()
    pltpu.make_async_remote_copy(
        src_ref=spans.at[pl.ds(0, SHARDS - 1)], dst_ref=spans.at[pl.ds(0, SHARDS - 1)],
        send_sem=span_send, recv_sem=span_recv, device_id={"ctx": lax.rem(me + 1, SHARDS)},
    ).wait()
    head = me // (SHARDS // HEADS)
    ends = [recv1[q].astype(F32) for q in range(SHARDS)]
    falls = [spans[q, pl.ds(head, 1)] for q in range(SHARDS)]
    for k in range(BITS):
        for group in range(0, len(ends), 2):
            left = ends[group].astype(BF16)
            for r in range((group + 1) << k, (group + 2) << k):
                stage[r * BITS + popcount(r % 2**k)] = left
        falls_next = [falls[i] + falls[i + 1] for i in range(0, len(falls), 2)]
        ends = [
            jnp.exp2(falls[i + 1]) * ends[i] + ends[i + 1] for i in range(0, len(ends), 2)
        ]
        falls = falls_next

    def answer(d, _):
        other = lax.rem(me + d, SHARDS)
        count = popcount(other)
        for n in range(1, BITS + 1):

            @pl.when(count == n)
            def _():
                pltpu.make_async_remote_copy(
                    src_ref=stage.at[pl.ds(other * BITS, n)],
                    dst_ref=recv3.at[pl.ds(me * BITS, n)],
                    send_sem=p3_send, recv_sem=p3_recv, device_id={"ctx": other},
                ).start()

        return 0

    lax.fori_loop(1, SHARDS, answer, 0)
    for n in range(1, BITS + 1):

        @pl.when(bits == n)
        def _():
            recv3[pl.ds(me * BITS, n)] = stage[pl.ds(me * BITS, n)]

    slot_weight[...] = jnp.zeros_like(slot_weight)
    for k in range(BITS):
        digit = (me // 2**k) % 2
        slot = popcount(me % 2**k)
        first = (me // 2**k) * 2**k

        @pl.when(digit == 1)
        def _():
            def add(q, total):
                return total + spans[q]

            between = lax.fori_loop(first, me, add, jnp.zeros((HEADS, HALF), F32))
            for c in range(PIECES):
                gap = between + jnp.zeros((HEADS, HALF), F32)
                for e in range(c):
                    gap = gap + jnp.broadcast_to(inner[e, :, STRETCH - 1 :], (HEADS, HALF))
                for half in range(2):
                    tokens = slice((2 * c + half) * HALF, (2 * c + half + 1) * HALF)
                    slot_weight[2 * c + half, slot] = level_ref[2 + k, :, tokens] * jnp.exp2(
                        gap + inner[c, :, half * HALF : (half + 1) * HALF]
                    )

    for n in range(1, BITS + 1):

        @pl.when(bits == n)
        def _():
            pltpu.make_async_remote_copy(
                src_ref=stage.at[pl.ds(0, (SHARDS - 1) * n)],
                dst_ref=recv3.at[pl.ds(0, (SHARDS - 1) * n)],
                send_sem=p3_send, recv_sem=p3_recv, device_id={"ctx": lax.rem(me + 1, SHARDS)},
            ).wait_recv()

    def finish(b, _):
        c, half = b // 2, b % 2
        q = qt[c, half]
        square = jnp.zeros((HEAD_DIM, HALF), F32)
        for h in range(HEADS):
            buckets = recv3[4 * BITS * h : 4 * BITS * (h + 1)].reshape(4 * BITS * ROWS, STATE)
            readout = jnp.dot(buckets, q, preferred_element_type=F32)
            weights = [slot_weight[b, j, h : h + 1] for j in range(BITS)]
            parts = []
            for piece in range(4):
                total = mixed[c, half, h * HEAD_DIM + piece * ROWS : h * HEAD_DIM + (piece + 1) * ROWS]
                for j in range(BITS):
                    at = (piece * BITS + j) * ROWS
                    total = total + readout[at : at + ROWS] * weights[j]
                parts.append(total)
            total = jnp.concatenate(parts, axis=0)
            mixed[c, half, h * HEAD_DIM : (h + 1) * HEAD_DIM] = total
            square = square + total * total
        mean = jnp.sum(square, axis=0, keepdims=True) * (1.0 / WIDTH)
        scale = lax.rsqrt(mean + 1e-05)
        for g in range(WIDTH // HALF):
            at = slice(g * HALF, (g + 1) * HALF)
            normed = (mixed[c, half, at] * scale * gain_col[at]).astype(BF16)
            out_ref[pl.ds(pl.multiple_of(b * HALF, HALF), HALF), at] = normed.T
        return 0

    lax.fori_loop(0, TOKENS // HALF, finish, 0)

    @pl.when(me < SHARDS - 1)
    def _():
        to_next.wait_send()

    for n in range(BITS + 1):

        @pl.when(bits == n)
        def _():
            pltpu.make_async_remote_copy(
                src_ref=stage.at[pl.ds(0, SHARDS * BITS // 2 - n)],
                dst_ref=recv3.at[pl.ds(0, SHARDS * BITS // 2 - n)],
                send_sem=p3_send, recv_sem=p3_recv, device_id={"ctx": lax.rem(me + 1, SHARDS)},
            ).wait_send()


def per_device(mixer_input, conv_weight, log_decay, level_weight, norm_gain):
    vmem = pl.BlockSpec(memory_space=pltpu.VMEM)
    return pl.pallas_call(
        kernel,
        out_shape=jax.ShapeDtypeStruct((TOKENS, WIDTH), BF16),
        in_specs=[vmem] * 5,
        out_specs=vmem,
        scratch_shapes=[
            pltpu.VMEM((16, WIDTH + 2 * STATE), BF16),
            pltpu.VMEM((PIECES, 2, WIDTH, HALF), BF16),
            pltpu.VMEM((PIECES, STRETCH, STATE), BF16),
            pltpu.VMEM((PIECES, 2, STATE, HALF), BF16),
            pltpu.VMEM((PIECES, HEADS, STRETCH), F32),
            pltpu.VMEM((PIECES, STRETCH, HEADS), F32),
            pltpu.VMEM((PIECES, WIDTH, STATE), F32),
            pltpu.VMEM((PIECES - 1, WIDTH, STATE), BF16),
            pltpu.VMEM((PIECES, 2, WIDTH, HALF), F32),
            pltpu.VMEM((WIDTH, 1), F32),
            pltpu.VMEM((TOKENS // HALF, BITS, HEADS, HALF), F32),
            pltpu.VMEM((SHARDS, ROWS, STATE), BF16),
            pltpu.VMEM((SHARDS, ROWS, STATE), BF16),
            pltpu.VMEM((HEADS, HALF), F32),
            pltpu.VMEM((SHARDS, HEADS, HALF), F32),
            pltpu.VMEM((SHARDS * BITS, ROWS, STATE), BF16),
            pltpu.VMEM((SHARDS * BITS, ROWS, STATE), BF16),
            pltpu.SemaphoreType.DMA((2,)),
            pltpu.SemaphoreType.DMA,
            pltpu.SemaphoreType.DMA,
            pltpu.SemaphoreType.DMA,
            pltpu.SemaphoreType.DMA,
            pltpu.SemaphoreType.DMA,
            pltpu.SemaphoreType.DMA,
        ],
        compiler_params=pltpu.CompilerParams(
            collective_id=0, has_side_effects=True, vmem_limit_bytes=40 << 20
        ),
    )(mixer_input, conv_weight, log_decay, level_weight, norm_gain.reshape(1, WIDTH))


def solution(mesh):
    placed = (
        P("ctx", "heads"),
        P(None, "heads"),
        P("heads", "ctx"),
        P(None, "heads", "ctx"),
        P("heads"),
    )
    return jax.shard_map(
        per_device, mesh=mesh, in_specs=placed, out_specs=P("ctx", "heads"), check_vma=False
    )
```

```python
import functools

import jax
import jax.numpy as jnp
from jax import lax
from jax.experimental import pallas as pl
from jax.experimental.pallas import tpu as pltpu
from jax.sharding import PartitionSpec as P

HEADS = 8
HEAD_DIM = 64
STATE = 128
STRETCH = 256
WIDTH = 512
TOKENS = 1024
PIECES = TOKENS // STRETCH
SHARDS = 32
ALONG_Z = 8
ALONG_Y = 4
BITS = 5
HALF = 128
GROUP = 16
ROWS = WIDTH // GROUP
MIDDLE = 3
LOG2E = 1.4426950408889634

NT = (((1,), (1,)), ((), ()))
F32 = jnp.float32
BF16 = jnp.bfloat16


def popcount(r):
    count = r % 2
    for k in range(1, BITS):
        count = count + (r // 2**k) % 2
    return count


def activate(window, conv_ref, cols):
    total = conv_ref[3:4, cols] * window[16:144]
    for j in range(3):
        total = total + conv_ref[j : j + 1, cols] * window[13 + j : 141 + j]
    half = 0.5 * total
    return (half + half * jnp.tanh(half)).astype(BF16)


def kernel(
    x_hbm, conv_hbm, rate_hbm, level_hbm, gain_hbm, out_ref,
    x_ref, conv_ref, rate_ref, level_ref, gain_ref, halo, xt, keys, qt, inner, column, state, low, mixed, gain_col, slot_weight,
    send1, recv1, spans, stage, top, recv3,
    in_sem, x_sem, halo_sem, p1_send, p1_recv, span_sem, p0_sem, p4_sem, p3_send, p3_recv,
):
    me = lax.axis_index("ctx")
    bits = popcount(me)
    pair = me // GROUP
    place_in = lax.rem(me, GROUP)
    odd = lax.rem(me, 2)
    middle = popcount(place_in // 2)

    barrier = pltpu.get_barrier_semaphore()

    small_in = [
        pltpu.make_async_copy(src, dst, in_sem.at[i])
        for i, (src, dst) in enumerate(
            ((rate_hbm, rate_ref), (conv_hbm, conv_ref), (gain_hbm, gain_ref), (level_hbm, level_ref))
        )
    ]

    def rows_in(start, count, at):
        span_of = pl.ds(start, count)
        return pltpu.make_async_copy(x_hbm.at[span_of], x_ref.at[span_of], x_sem.at[at])

    def stretch_in(c):
        return rows_in(pl.multiple_of(c * STRETCH - 16, 16), STRETCH, c)

    head_in = rows_in(0, STRETCH - 16, 0)
    tail_in = rows_in(TOKENS - 16, 16, PIECES)
    for copy in small_in[:3]:
        copy.start()
    tail_in.start()
    for c in range(PIECES - 1, 0, -1):
        stretch_in(c).start()
    head_in.start()
    small_in[3].start()

    def greet(d, _):
        other = lax.rem(me + d, SHARDS)
        pl.semaphore_signal(barrier, inc=1, device_id={"ctx": other})
        return 0

    lax.fori_loop(1, SHARDS, greet, 0)

    small_in[0].wait()
    rows = lax.broadcasted_iota(jnp.int32, (STRETCH, STRETCH), 0)
    cols = lax.broadcasted_iota(jnp.int32, (STRETCH, STRETCH), 1)
    lower = jnp.where(rows >= cols, 1.0, 0.0).astype(F32)
    span = jnp.zeros((HEADS, HALF), F32)
    for c in range(PIECES):
        rate = rate_ref[:, c * STRETCH : (c + 1) * STRETCH] * LOG2E
        inner[c] = lax.dot_general(
            rate, lower, NT, precision=lax.Precision.HIGHEST, preferred_element_type=F32
        )
        column[c] = lax.dot_general(
            lower, rate, NT, precision=lax.Precision.HIGHEST, preferred_element_type=F32
        )
        span = span + jnp.broadcast_to(inner[c, :, STRETCH - 1 :], (HEADS, HALF))
    spans[me] = span

    small_in[1].wait()
    small_in[2].wait()
    diag = (rows == cols)[:HALF, :HALF]
    for g in range(WIDTH // HALF):
        row = jnp.broadcast_to(gain_ref[:, g * HALF : (g + 1) * HALF], (HALF, HALF))
        gain_col[g * HALF : (g + 1) * HALF] = jnp.sum(
            jnp.where(diag, row, 0.0), axis=1, keepdims=True
        )

    row_start = me - lax.rem(me, ALONG_Z)

    def to_row(d):
        return row_start + lax.rem(me + d, ALONG_Z)

    def to_column(d):
        return lax.rem(me + d * ALONG_Z, SHARDS)

    def span_along_row(d):
        return pltpu.make_async_remote_copy(
            src_ref=spans.at[me], dst_ref=spans.at[me],
            send_sem=span_sem.at[0], recv_sem=span_sem.at[1], device_id={"ctx": to_row(d)},
        )

    def span_along_column(d):
        at = pl.ds(row_start, ALONG_Z)
        return pltpu.make_async_remote_copy(
            src_ref=spans.at[at], dst_ref=spans.at[at],
            send_sem=span_sem.at[2], recv_sem=span_sem.at[3], device_id={"ctx": to_column(d)},
        )

    def wait_bytes(ref, count, send_sem, recv_sem):
        part = ref.at[pl.ds(0, count)]
        return pltpu.make_async_remote_copy(
            src_ref=part, dst_ref=part, send_sem=send_sem, recv_sem=recv_sem,
            device_id={"ctx": lax.rem(me + 1, SHARDS)},
        )

    to_next = pltpu.make_async_remote_copy(
        src_ref=x_hbm.at[pl.ds(TOKENS - 16, 16)], dst_ref=halo,
        send_sem=halo_sem.at[0], recv_sem=halo_sem.at[1],
        device_id={"ctx": lax.rem(me + 1, SHARDS)},
    )

    def place(b, group, act):
        c, half = b // 2, b % 2
        if group < 4:
            xt[c, half, group * HALF : (group + 1) * HALF] = act.T
        elif group == 4:
            keys[c, pl.ds(pl.multiple_of(half * HALF, HALF), HALF)] = act
        else:
            qt[c, half] = act.T

    def block(b):
        start = pl.multiple_of(b * HALF - 16, 16)
        for group in range(6):
            chans = slice(group * HALF, (group + 1) * HALF)
            window = x_ref[pl.ds(start, HALF + 16), chans].astype(F32)
            place(b, group, activate(window, conv_ref, chans))

    def stretch_state(c):
        to_end = jnp.exp2(inner[c, :, STRETCH - 1 :] - inner[c])
        parts = []
        for h in range(HEADS):
            x_h = jnp.concatenate(
                [xt[c, 0, h * HEAD_DIM : (h + 1) * HEAD_DIM], xt[c, 1, h * HEAD_DIM : (h + 1) * HEAD_DIM]],
                axis=1,
            )
            parts.append((x_h.astype(F32) * to_end[h : h + 1]).astype(BF16))
        state[c] = jnp.dot(
            jnp.concatenate(parts, axis=0), keys[c], preferred_element_type=F32
        )

    tail_in.wait()

    def late(i, _):
        c = PIECES - 1 - i
        stretch_in(c).wait()
        lax.fori_loop(0, 2, lambda half, _: (block(2 * c + 1 - half), 0)[1], 0)
        stretch_state(c)

        @pl.when(i == 0)
        def _():
            pl.semaphore_wait(barrier, SHARDS - 1)

            @pl.when(me < SHARDS - 1)
            def _():
                to_next.start()

            for d in range(1, ALONG_Z):
                span_along_row(d).start()

        return 0

    lax.fori_loop(0, PIECES - 1, late, 0)
    head_in.wait()
    block(1)

    @pl.when(me == 0)
    def _():
        halo[...] = jnp.zeros_like(halo)

    @pl.when(me > 0)
    def _():
        to_next.wait_recv()


    for group in range(6):
        chans = slice(group * HALF, (group + 1) * HALF)
        window = jnp.concatenate([halo[:, chans], x_ref[:HALF, chans]], axis=0).astype(F32)
        place(0, group, activate(window, conv_ref, chans))
    stretch_state(0)

    for h in range(HEADS):
        at = slice(h * HEAD_DIM, (h + 1) * HEAD_DIM)
        carried = state[0, at]
        for c in range(1, PIECES):
            low[c - 1, at] = carried.astype(BF16)
            fall = jnp.exp2(
                jnp.broadcast_to(inner[c, h : h + 1, STRETCH - 1 :], (1, STATE))
            )
            carried = fall * carried + state[c, at]
        send1[2 * h : 2 * (h + 1)] = carried.astype(BF16).reshape(2, ROWS, STATE)

    def spread(d, _):
        there = lax.rem(place_in + d, GROUP)
        pltpu.make_async_remote_copy(
            src_ref=send1.at[there], dst_ref=recv1.at[place_in],
            send_sem=p1_send, recv_sem=p1_recv, device_id={"ctx": pair * GROUP + there},
        ).start()
        return 0

    lax.fori_loop(1, GROUP, spread, 0)
    recv1[place_in] = send1[place_in]

    causal = (rows <= cols)[:HALF, :HALF]

    def near_own(c, before):
        q = [qt[c, 0], qt[c, 1]]
        k = keys[c]
        for half in range(2):
            width = HALF * (half + 1)
            score = jnp.dot(k[:width], q[half], preferred_element_type=F32)
            at_t = pl.ds(pl.multiple_of(c * STRETCH, STRETCH) + half * HALF, HALF)
            row_all = inner[c, :, half * HALF : (half + 1) * HALF]
            own_scale = level_ref[0, :, at_t]
            near_scale = level_ref[1, :, at_t] * jnp.exp2(row_all)
            if before:
                readout = jnp.dot(low[c - 1], q[half], preferred_element_type=F32)
            for h in range(HEADS):
                at = slice(h * HEAD_DIM, (h + 1) * HEAD_DIM)
                gap = row_all[h : h + 1] - column[c, :width, h : h + 1]
                blocks = []
                if half == 1:
                    blocks.append((jnp.exp2(gap[:HALF]) * score[:HALF]).astype(BF16))
                last = jnp.where(causal, gap[width - HALF :], -jnp.inf)
                blocks.append((jnp.exp2(last) * score[width - HALF :]).astype(BF16))
                own = jnp.dot(xt[c, half, at], blocks[-1], preferred_element_type=F32)
                if half == 1:
                    own = own + jnp.dot(xt[c, 0, at], blocks[0], preferred_element_type=F32)
                own = own * own_scale[h : h + 1]
                if before:
                    own = own + readout[at] * near_scale[h : h + 1]
                mixed[c, half, at] = own

    small_in[3].wait()
    near_own(0, False)
    wait_bytes(spans, ALONG_Z - 1, span_sem.at[0], span_sem.at[1]).wait()
    for d in range(1, ALONG_Y):
        span_along_column(d).start()

    neighbour = pltpu.make_async_remote_copy(
        src_ref=send1, dst_ref=recv3.at[pair],
        send_sem=p0_sem.at[0], recv_sem=p0_sem.at[1],
        device_id={"ctx": lax.rem(me + 1, SHARDS)},
    )

    def rest(c, _):
        near_own(c, True)

        @pl.when((odd == 0) & (c == 1))
        def _():
            neighbour.start()

        return 0

    lax.fori_loop(1, PIECES, rest, 0)

    wait_bytes(recv1, GROUP - 1, p1_send, p1_recv).wait()
    wait_bytes(spans, SHARDS - ALONG_Z, span_sem.at[2], span_sem.at[3]).wait()
    head = place_in // (GROUP // HEADS)
    ends = [recv1[q].astype(F32) for q in range(GROUP)]
    falls = [spans[pair * GROUP + q, pl.ds(head, 1)] for q in range(GROUP)]
    for k in range(BITS - 1):
        if k > 0:
            for group in range(0, len(ends), 2):
                left = ends[group].astype(BF16)
                for r in range((group + 1) << k, (group + 2) << k):
                    stage[popcount((r // 2) % 2 ** (k - 1)), r] = left
        ends = [
            jnp.exp2(falls[i + 1]) * ends[i] + ends[i + 1] for i in range(0, len(ends), 2)
        ]
        falls = [falls[i] + falls[i + 1] for i in range(0, len(falls), 2)]
    top[...] = ends[0].astype(BF16)

    def answer(i, _):
        early = jnp.where(i < 4, 1, 0)
        turn = lax.rem(place_in + i, 4) * early + lax.rem(place_in + i, 12) * (1 - early)
        there = early * ((turn // 2) * ALONG_Z + turn % 2) + (1 - early) * ((turn // 6) * ALONG_Z + 2 + turn % 6)
        @pl.when(pair == 0)
        def _():
            pltpu.make_async_remote_copy(
                src_ref=top, dst_ref=recv3.at[0, place_in],
                send_sem=p4_sem.at[0], recv_sem=p4_sem.at[1],
                device_id={"ctx": GROUP + there},
            ).start()

        count = popcount(there // 2) * jnp.where(there == place_in, 0, 1)
        for n in range(1, MIDDLE + 1):

            @pl.when(count == n)
            def _():
                pltpu.make_async_remote_copy(
                    src_ref=stage.at[pl.ds(0, n), there],
                    dst_ref=recv3.at[pl.ds(pair + lax.rem(there, 2), n), place_in],
                    send_sem=p3_send, recv_sem=p3_recv,
                    device_id={"ctx": pair * GROUP + there},
                ).start()

        return 0

    lax.fori_loop(0, GROUP, answer, 0)
    for n in range(1, MIDDLE + 1):

        @pl.when(middle == n)
        def _():
            recv3[pl.ds(pair + odd, n), place_in] = stage[:n, place_in]

    for k in range(BITS):
        digit = (me // 2**k) % 2
        if k == 0:
            slot = pair
        elif k == BITS - 1:
            slot = 0
        else:
            slot = pair + odd + popcount((me // 2) % 2 ** (k - 1))
        first = (me // 2**k) * 2**k

        @pl.when(digit == 1)
        def _():
            def add(q, total):
                return total + spans[q]

            between = lax.fori_loop(first, me, add, jnp.zeros((HEADS, HALF), F32))
            for c in range(PIECES):
                gap = between + jnp.zeros((HEADS, HALF), F32)
                for e in range(c):
                    gap = gap + jnp.broadcast_to(inner[e, :, STRETCH - 1 :], (HEADS, HALF))
                for half in range(2):
                    tokens = slice((2 * c + half) * HALF, (2 * c + half + 1) * HALF)
                    slot_weight[2 * c + half, slot] = level_ref[2 + k, :, tokens] * jnp.exp2(
                        gap + inner[c, :, half * HALF : (half + 1) * HALF]
                    )

    @pl.when(odd == 1)
    def _():
        neighbour.wait_recv()

    for n in range(1, MIDDLE + 1):

        @pl.when(middle == n)
        def _():
            part = recv3.at[pl.ds(0, n), pl.ds(0, GROUP - 1)]
            pltpu.make_async_remote_copy(
                src_ref=part, dst_ref=part, send_sem=p3_send, recv_sem=p3_recv,
                device_id={"ctx": lax.rem(me + 1, SHARDS)},
            ).wait_recv()

    @pl.when(pair == 1)
    def _():
        wait_bytes(recv1, GROUP, p4_sem.at[0], p4_sem.at[1]).wait_recv()

    def finish(c, _):
        q = jnp.concatenate([qt[c, 0], qt[c, 1]], axis=1)

        def add_bucket(j, _):
            for g in range(4):
                bucket = recv3[j, g * 4 : (g + 1) * 4].reshape(HALF, STATE)
                readout = jnp.dot(bucket, q, preferred_element_type=F32)
                for half in range(2):
                    lanes = slice(half * HALF, (half + 1) * HALF)
                    for h in range(2):
                        at = slice(h * HEAD_DIM, (h + 1) * HEAD_DIM)
                        to = slice(g * HALF + h * HEAD_DIM, g * HALF + (h + 1) * HEAD_DIM)
                        weight = slot_weight[2 * c + half, j, 2 * g + h : 2 * g + h + 1]
                        mixed[c, half, to] = mixed[c, half, to] + readout[at, lanes] * weight
            return 0

        lax.fori_loop(0, bits, add_bucket, 0)
        for half in range(2):
            square = jnp.zeros((HEAD_DIM, HALF), F32)
            for h in range(HEADS):
                part = mixed[c, half, h * HEAD_DIM : (h + 1) * HEAD_DIM]
                square = square + part * part
            mean = jnp.sum(square, axis=0, keepdims=True) * (1.0 / WIDTH)
            scale = lax.rsqrt(mean + 1e-05)
            for g in range(WIDTH // HALF):
                at = slice(g * HALF, (g + 1) * HALF)
                normed = (mixed[c, half, at] * scale * gain_col[at]).astype(BF16)
                tokens = pl.ds(pl.multiple_of(c * STRETCH, STRETCH) + half * HALF, HALF)
                out_ref[tokens, at] = normed.T
        return 0

    lax.fori_loop(0, PIECES, finish, 0)

    @pl.when(me < SHARDS - 1)
    def _():
        to_next.wait_send()

    @pl.when(odd == 0)
    def _():
        neighbour.wait_send()

    @pl.when(pair == 0)
    def _():
        wait_bytes(recv1, GROUP, p4_sem.at[0], p4_sem.at[1]).wait_send()

    for n in range(MIDDLE + 1):

        @pl.when(middle == n)
        def _():
            for part in (stage.at[0], stage.at[1, pl.ds(0, GROUP // 2 - n)]):
                pltpu.make_async_remote_copy(
                    src_ref=part, dst_ref=part, send_sem=p3_send, recv_sem=p3_recv,
                    device_id={"ctx": lax.rem(me + 1, SHARDS)},
                ).wait_send()


def per_device(mixer_input, conv_weight, log_decay, level_weight, norm_gain):
    vmem = pl.BlockSpec(memory_space=pltpu.VMEM)
    hbm = pl.BlockSpec(memory_space=pltpu.HBM)
    return pl.pallas_call(
        kernel,
        out_shape=jax.ShapeDtypeStruct((TOKENS, WIDTH), BF16),
        in_specs=[hbm] * 5,
        out_specs=vmem,
        scratch_shapes=[
            pltpu.VMEM((TOKENS, WIDTH + 2 * STATE), BF16),
            pltpu.VMEM((4, WIDTH + 2 * STATE), F32),
            pltpu.VMEM((HEADS, TOKENS), F32),
            pltpu.VMEM((2 + BITS, HEADS, TOKENS), F32),
            pltpu.VMEM((1, WIDTH), F32),
            pltpu.VMEM((16, WIDTH + 2 * STATE), BF16),
            pltpu.VMEM((PIECES, 2, WIDTH, HALF), BF16),
            pltpu.VMEM((PIECES, STRETCH, STATE), BF16),
            pltpu.VMEM((PIECES, 2, STATE, HALF), BF16),
            pltpu.VMEM((PIECES, HEADS, STRETCH), F32),
            pltpu.VMEM((PIECES, STRETCH, HEADS), F32),
            pltpu.VMEM((PIECES, WIDTH, STATE), F32),
            pltpu.VMEM((PIECES - 1, WIDTH, STATE), BF16),
            pltpu.VMEM((PIECES, 2, WIDTH, HALF), F32),
            pltpu.VMEM((WIDTH, 1), F32),
            pltpu.VMEM((TOKENS // HALF, BITS, HEADS, HALF), F32),
            pltpu.VMEM((GROUP, ROWS, STATE), BF16),
            pltpu.VMEM((GROUP, ROWS, STATE), BF16),
            pltpu.VMEM((SHARDS, HEADS, HALF), F32),
            pltpu.VMEM((MIDDLE, GROUP, ROWS, STATE), BF16),
            pltpu.VMEM((ROWS, STATE), BF16),
            pltpu.VMEM((BITS, GROUP, ROWS, STATE), BF16),
            pltpu.SemaphoreType.DMA((4,)),
            pltpu.SemaphoreType.DMA((PIECES + 1,)),
            pltpu.SemaphoreType.DMA((2,)),
            pltpu.SemaphoreType.DMA,
            pltpu.SemaphoreType.DMA,
            pltpu.SemaphoreType.DMA((4,)),
            pltpu.SemaphoreType.DMA((2,)),
            pltpu.SemaphoreType.DMA((2,)),
            pltpu.SemaphoreType.DMA,
            pltpu.SemaphoreType.DMA,
        ],
        compiler_params=pltpu.CompilerParams(
            collective_id=0, has_side_effects=True, vmem_limit_bytes=63 << 20
        ),
    )(mixer_input, conv_weight, log_decay, level_weight, norm_gain.reshape(1, WIDTH))


def solution(mesh):
    placed = (
        P("ctx", "heads"),
        P(None, "heads"),
        P("heads", "ctx"),
        P(None, "heads", "ctx"),
        P("heads"),
    )
    return jax.shard_map(
        per_device, mesh=mesh, in_specs=placed, out_specs=P("ctx", "heads"), check_vma=False
    )
```

```python
import functools

import jax
import jax.numpy as jnp
from jax import lax
from jax.experimental import pallas as pl
from jax.experimental.pallas import tpu as pltpu
from jax.sharding import PartitionSpec as P

HEADS = 8
HEAD_DIM = 64
STATE = 128
STRETCH = 256
WIDTH = 512
TOKENS = 1024
PIECES = TOKENS // STRETCH
SHARDS = 32
ALONG_Z = 8
ALONG_Y = 4
BITS = 5
HALF = 128
GROUP = 16
ROWS = WIDTH // GROUP
MIDDLE = 3
LOG2E = 1.4426950408889634

NT = (((1,), (1,)), ((), ()))
F32 = jnp.float32
BF16 = jnp.bfloat16


def popcount(r):
    count = r % 2
    for k in range(1, BITS):
        count = count + (r // 2**k) % 2
    return count


def activate(window, conv_ref, cols):
    total = conv_ref[3:4, cols] * window[16:144]
    for j in range(3):
        total = total + conv_ref[j : j + 1, cols] * window[13 + j : 141 + j]
    half = 0.5 * total
    return (half + half * jnp.tanh(half)).astype(BF16)


def kernel(
    x_hbm, conv_hbm, rate_hbm, level_hbm, gain_hbm, out_hbm,
    out_ref, x_ref, conv_ref, rate_ref, level_ref, gain_ref, halo, xt, keys, qt, inner, column, state, low, mixed, gain_col, slot_weight,
    send1, recv1, spans, stage, top, recv3,
    in_sem, x_sem, out_sem, halo_sem, p1_send, p1_recv, span_sem, p0_sem, p4_sem, p3_send, p3_recv,
):
    me = lax.axis_index("ctx")
    bits = popcount(me)
    pair = me // GROUP
    place_in = lax.rem(me, GROUP)
    odd = lax.rem(me, 2)
    middle = popcount(place_in // 2)

    barrier = pltpu.get_barrier_semaphore()

    small_in = [
        pltpu.make_async_copy(src, dst, in_sem.at[i])
        for i, (src, dst) in enumerate(
            ((rate_hbm, rate_ref), (conv_hbm, conv_ref), (gain_hbm, gain_ref), (level_hbm, level_ref))
        )
    ]

    def rows_in(start, count, at):
        span_of = pl.ds(start, count)
        return pltpu.make_async_copy(x_hbm.at[span_of], x_ref.at[span_of], x_sem.at[at])

    def stretch_in(c):
        return rows_in(pl.multiple_of(c * STRETCH - 16, 16), STRETCH, c)

    head_in = rows_in(0, STRETCH - 16, 0)
    tail_in = rows_in(TOKENS - 16, 16, PIECES)
    for copy in small_in[:3]:
        copy.start()
    tail_in.start()
    for c in range(PIECES - 1, 0, -1):
        stretch_in(c).start()
    head_in.start()
    small_in[3].start()

    def greet(d, _):
        other = lax.rem(me + d, SHARDS)
        pl.semaphore_signal(barrier, inc=1, device_id={"ctx": other})
        return 0

    lax.fori_loop(1, SHARDS, greet, 0)

    small_in[0].wait()
    rows = lax.broadcasted_iota(jnp.int32, (STRETCH, STRETCH), 0)
    cols = lax.broadcasted_iota(jnp.int32, (STRETCH, STRETCH), 1)
    lower = jnp.where(rows >= cols, 1.0, 0.0).astype(F32)
    rates = jnp.concatenate(
        [rate_ref[:, c * STRETCH : (c + 1) * STRETCH] for c in range(PIECES)], axis=0
    )
    sums = lax.dot_general(
        rates * LOG2E, lower, NT, precision=lax.Precision.HIGHEST, preferred_element_type=F32
    )
    span = jnp.zeros((HEADS, HALF), F32)
    for c in range(PIECES):
        part = sums[c * HEADS : (c + 1) * HEADS]
        inner[c] = part
        span = span + jnp.broadcast_to(part[:, STRETCH - 1 :], (HEADS, HALF))
    spans[me] = span
    small_in[1].wait()

    row_start = me - lax.rem(me, ALONG_Z)

    def to_row(d):
        return row_start + lax.rem(me + d, ALONG_Z)

    def to_column(d):
        return lax.rem(me + d * ALONG_Z, SHARDS)

    def span_along_row(d):
        return pltpu.make_async_remote_copy(
            src_ref=spans.at[me], dst_ref=spans.at[me],
            send_sem=span_sem.at[0], recv_sem=span_sem.at[1], device_id={"ctx": to_row(d)},
        )

    def span_along_column(d):
        at = pl.ds(row_start, ALONG_Z)
        return pltpu.make_async_remote_copy(
            src_ref=spans.at[at], dst_ref=spans.at[at],
            send_sem=span_sem.at[2], recv_sem=span_sem.at[3], device_id={"ctx": to_column(d)},
        )

    def wait_bytes(ref, count, send_sem, recv_sem):
        part = ref.at[pl.ds(0, count)]
        return pltpu.make_async_remote_copy(
            src_ref=part, dst_ref=part, send_sem=send_sem, recv_sem=recv_sem,
            device_id={"ctx": lax.rem(me + 1, SHARDS)},
        )

    to_next = pltpu.make_async_remote_copy(
        src_ref=x_hbm.at[pl.ds(TOKENS - 16, 16)], dst_ref=halo,
        send_sem=halo_sem.at[0], recv_sem=halo_sem.at[1],
        device_id={"ctx": lax.rem(me + 1, SHARDS)},
    )

    def place(b, group, act):
        c, half = b // 2, b % 2
        if group < 4:
            xt[c, half, group * HALF : (group + 1) * HALF] = act.T
        elif group == 4:
            keys[c, pl.ds(pl.multiple_of(half * HALF, HALF), HALF)] = act
        else:
            qt[c, half] = act.T

    def block(b):
        start = pl.multiple_of(b * HALF - 16, 16)
        for group in range(6):
            chans = slice(group * HALF, (group + 1) * HALF)
            window = x_ref[pl.ds(start, HALF + 16), chans].astype(F32)
            place(b, group, activate(window, conv_ref, chans))

    def stretch_state(c):
        to_end = jnp.exp2(inner[c, :, STRETCH - 1 :] - inner[c])
        parts = []
        for h in range(HEADS):
            x_h = jnp.concatenate(
                [xt[c, 0, h * HEAD_DIM : (h + 1) * HEAD_DIM], xt[c, 1, h * HEAD_DIM : (h + 1) * HEAD_DIM]],
                axis=1,
            )
            parts.append((x_h.astype(F32) * to_end[h : h + 1]).astype(BF16))
        state[c] = jnp.dot(
            jnp.concatenate(parts, axis=0), keys[c], preferred_element_type=F32
        )

    tail_in.wait()

    def late(i, _):
        c = PIECES - 1 - i
        stretch_in(c).wait()
        lax.fori_loop(0, 2, lambda half, _: (block(2 * c + 1 - half), 0)[1], 0)
        stretch_state(c)

        @pl.when(i == 0)
        def _():
            pl.semaphore_wait(barrier, SHARDS - 1)

            @pl.when(me < SHARDS - 1)
            def _():
                to_next.start()

            for d in range(1, ALONG_Z):
                span_along_row(d).start()

        return 0

    lax.fori_loop(0, PIECES - 1, late, 0)
    head_in.wait()
    block(1)

    @pl.when(me == 0)
    def _():
        halo[...] = jnp.zeros_like(halo)

    @pl.when(me > 0)
    def _():
        to_next.wait_recv()


    for group in range(6):
        chans = slice(group * HALF, (group + 1) * HALF)
        window = jnp.concatenate([halo[:, chans], x_ref[:HALF, chans]], axis=0).astype(F32)
        place(0, group, activate(window, conv_ref, chans))
    stretch_state(0)

    for h in range(HEADS):
        at = slice(h * HEAD_DIM, (h + 1) * HEAD_DIM)
        carried = state[0, at]
        for c in range(1, PIECES):
            low[c - 1, at] = carried.astype(BF16)
            fall = jnp.exp2(
                jnp.broadcast_to(inner[c, h : h + 1, STRETCH - 1 :], (1, STATE))
            )
            carried = fall * carried + state[c, at]
        send1[2 * h : 2 * (h + 1)] = carried.astype(BF16).reshape(2, ROWS, STATE)

    def spread(d, _):
        there = lax.rem(place_in + d, GROUP)
        pltpu.make_async_remote_copy(
            src_ref=send1.at[there], dst_ref=recv1.at[place_in],
            send_sem=p1_send, recv_sem=p1_recv, device_id={"ctx": pair * GROUP + there},
        ).start()
        return 0

    lax.fori_loop(1, GROUP, spread, 0)
    recv1[place_in] = send1[place_in]

    small_in[2].wait()
    diag = (rows == cols)[:HALF, :HALF]
    for g in range(WIDTH // HALF):
        row = jnp.broadcast_to(gain_ref[:, g * HALF : (g + 1) * HALF], (HALF, HALF))
        gain_col[g * HALF : (g + 1) * HALF] = jnp.sum(
            jnp.where(diag, row, 0.0), axis=1, keepdims=True
        )
    for c in range(PIECES):
        rate = rate_ref[:, c * STRETCH : (c + 1) * STRETCH] * LOG2E
        column[c] = lax.dot_general(
            lower, rate, NT, precision=lax.Precision.HIGHEST, preferred_element_type=F32
        )
    causal = (rows <= cols)[:HALF, :HALF]

    def near_own(c, before):
        q = [qt[c, 0], qt[c, 1]]
        k = keys[c]
        for half in range(2):
            width = HALF * (half + 1)
            score = jnp.dot(k[:width], q[half], preferred_element_type=F32)
            at_t = pl.ds(pl.multiple_of(c * STRETCH, STRETCH) + half * HALF, HALF)
            row_all = inner[c, :, half * HALF : (half + 1) * HALF]
            own_scale = level_ref[0, :, at_t]
            near_scale = level_ref[1, :, at_t] * jnp.exp2(row_all)
            if before:
                readout = jnp.dot(low[c - 1], q[half], preferred_element_type=F32)
            for h in range(HEADS):
                at = slice(h * HEAD_DIM, (h + 1) * HEAD_DIM)
                gap = row_all[h : h + 1] - column[c, :width, h : h + 1]
                blocks = []
                if half == 1:
                    blocks.append((jnp.exp2(gap[:HALF]) * score[:HALF]).astype(BF16))
                last = jnp.where(causal, gap[width - HALF :], -jnp.inf)
                blocks.append((jnp.exp2(last) * score[width - HALF :]).astype(BF16))
                own = jnp.dot(xt[c, half, at], blocks[-1], preferred_element_type=F32)
                if half == 1:
                    own = own + jnp.dot(xt[c, 0, at], blocks[0], preferred_element_type=F32)
                own = own * own_scale[h : h + 1]
                if before:
                    own = own + readout[at] * near_scale[h : h + 1]
                mixed[c, half, at] = own

    small_in[3].wait()
    near_own(0, False)
    wait_bytes(spans, ALONG_Z - 1, span_sem.at[0], span_sem.at[1]).wait()
    for d in range(1, ALONG_Y):
        span_along_column(d).start()

    neighbour = pltpu.make_async_remote_copy(
        src_ref=send1, dst_ref=recv3.at[pair],
        send_sem=p0_sem.at[0], recv_sem=p0_sem.at[1],
        device_id={"ctx": lax.rem(me + 1, SHARDS)},
    )

    def rest(c, _):
        near_own(c, True)

        @pl.when((odd == 0) & (c == 1))
        def _():
            neighbour.start()

        return 0

    lax.fori_loop(1, PIECES, rest, 0)

    wait_bytes(recv1, GROUP - 1, p1_send, p1_recv).wait()
    wait_bytes(spans, SHARDS - ALONG_Z, span_sem.at[2], span_sem.at[3]).wait()
    head = place_in // (GROUP // HEADS)
    ends = [recv1[q].astype(F32) for q in range(GROUP)]
    falls = [spans[pair * GROUP + q, pl.ds(head, 1)] for q in range(GROUP)]
    for k in range(BITS - 1):
        if k > 0:
            for group in range(0, len(ends), 2):
                left = ends[group].astype(BF16)
                for r in range((group + 1) << k, (group + 2) << k):
                    stage[popcount((r // 2) % 2 ** (k - 1)), r] = left
        ends = [
            jnp.exp2(falls[i + 1]) * ends[i] + ends[i + 1] for i in range(0, len(ends), 2)
        ]
        falls = [falls[i] + falls[i + 1] for i in range(0, len(falls), 2)]
    top[...] = ends[0].astype(BF16)

    def answer(i, _):
        early = jnp.where(i < 4, 1, 0)
        turn = lax.rem(place_in + i, 4) * early + lax.rem(place_in + i, 12) * (1 - early)
        there = early * ((turn // 2) * ALONG_Z + turn % 2) + (1 - early) * ((turn // 6) * ALONG_Z + 2 + turn % 6)
        @pl.when(pair == 0)
        def _():
            pltpu.make_async_remote_copy(
                src_ref=top, dst_ref=recv3.at[0, place_in],
                send_sem=p4_sem.at[0], recv_sem=p4_sem.at[1],
                device_id={"ctx": GROUP + there},
            ).start()

        count = popcount(there // 2) * jnp.where(there == place_in, 0, 1)
        for n in range(1, MIDDLE + 1):

            @pl.when(count == n)
            def _():
                pltpu.make_async_remote_copy(
                    src_ref=stage.at[pl.ds(0, n), there],
                    dst_ref=recv3.at[pl.ds(pair + lax.rem(there, 2), n), place_in],
                    send_sem=p3_send, recv_sem=p3_recv,
                    device_id={"ctx": pair * GROUP + there},
                ).start()

        return 0

    lax.fori_loop(0, GROUP, answer, 0)
    for n in range(1, MIDDLE + 1):

        @pl.when(middle == n)
        def _():
            recv3[pl.ds(pair + odd, n), place_in] = stage[:n, place_in]

    for k in range(BITS):
        digit = (me // 2**k) % 2
        if k == 0:
            slot = pair
        elif k == BITS - 1:
            slot = 0
        else:
            slot = pair + odd + popcount((me // 2) % 2 ** (k - 1))
        first = (me // 2**k) * 2**k

        @pl.when(digit == 1)
        def _():
            def add(q, total):
                return total + spans[q]

            between = lax.fori_loop(first, me, add, jnp.zeros((HEADS, HALF), F32))
            for c in range(PIECES):
                gap = between + jnp.zeros((HEADS, HALF), F32)
                for e in range(c):
                    gap = gap + jnp.broadcast_to(inner[e, :, STRETCH - 1 :], (HEADS, HALF))
                for half in range(2):
                    tokens = slice((2 * c + half) * HALF, (2 * c + half + 1) * HALF)
                    slot_weight[2 * c + half, slot] = level_ref[2 + k, :, tokens] * jnp.exp2(
                        gap + inner[c, :, half * HALF : (half + 1) * HALF]
                    )

    def add_bucket(i, _):
        slot = lax.rem(pair + i, bits)

        @pl.when((odd == 1) & (i == 0))
        def _():
            neighbour.wait_recv()

        for n in range(1, MIDDLE + 1):

            @pl.when((middle == n) & (i == odd))
            def _():
                part = recv3.at[pl.ds(0, n), pl.ds(0, GROUP - 1)]
                pltpu.make_async_remote_copy(
                    src_ref=part, dst_ref=part, send_sem=p3_send, recv_sem=p3_recv,
                    device_id={"ctx": lax.rem(me + 1, SHARDS)},
                ).wait_recv()

        @pl.when((pair == 1) & (i == bits - 1))
        def _():
            wait_bytes(recv1, GROUP, p4_sem.at[0], p4_sem.at[1]).wait_recv()

        for c in range(PIECES):
            q = jnp.concatenate([qt[c, 0], qt[c, 1]], axis=1)
            for g in range(4):
                bucket = recv3[slot, g * 4 : (g + 1) * 4].reshape(HALF, STATE)
                readout = jnp.dot(bucket, q, preferred_element_type=F32)
                for half in range(2):
                    lanes = slice(half * HALF, (half + 1) * HALF)
                    for h in range(2):
                        at = slice(h * HEAD_DIM, (h + 1) * HEAD_DIM)
                        to = slice(g * HALF + h * HEAD_DIM, g * HALF + (h + 1) * HEAD_DIM)
                        weight = slot_weight[2 * c + half, slot, 2 * g + h : 2 * g + h + 1]
                        mixed[c, half, to] = mixed[c, half, to] + readout[at, lanes] * weight
        return 0

    lax.fori_loop(0, bits, add_bucket, 0)

    def tokens_out(b):
        return pltpu.make_async_copy(out_ref.at[b], out_hbm.at[b], out_sem.at[b])

    for b in range(TOKENS // HALF):
        c, half = b // 2, b % 2
        square = jnp.zeros((HEAD_DIM, HALF), F32)
        for h in range(HEADS):
            part = mixed[c, half, h * HEAD_DIM : (h + 1) * HEAD_DIM]
            square = square + part * part
        mean = jnp.sum(square, axis=0, keepdims=True) * (1.0 / WIDTH)
        scale = lax.rsqrt(mean + 1e-05)
        out_ref[b] = (mixed[c, half] * scale * gain_col[...]).astype(BF16)
        tokens_out(b).start()

    @pl.when(me < SHARDS - 1)
    def _():
        to_next.wait_send()

    @pl.when(odd == 0)
    def _():
        neighbour.wait_send()

    @pl.when(pair == 0)
    def _():
        wait_bytes(recv1, GROUP, p4_sem.at[0], p4_sem.at[1]).wait_send()

    for n in range(MIDDLE + 1):

        @pl.when(middle == n)
        def _():
            for part in (stage.at[0], stage.at[1, pl.ds(0, GROUP // 2 - n)]):
                pltpu.make_async_remote_copy(
                    src_ref=part, dst_ref=part, send_sem=p3_send, recv_sem=p3_recv,
                    device_id={"ctx": lax.rem(me + 1, SHARDS)},
                ).wait_send()

    for b in range(TOKENS // HALF):
        tokens_out(b).wait()


def per_device(mixer_input, conv_weight, log_decay, level_weight, norm_gain):
    hbm = pl.BlockSpec(memory_space=pltpu.HBM)
    blocks = pl.pallas_call(
        kernel,
        out_shape=jax.ShapeDtypeStruct((TOKENS // HALF, WIDTH, HALF), BF16),
        in_specs=[hbm] * 5,
        out_specs=hbm,
        scratch_shapes=[
            pltpu.VMEM((TOKENS // HALF, WIDTH, HALF), BF16),
            pltpu.VMEM((TOKENS, WIDTH + 2 * STATE), BF16),
            pltpu.VMEM((4, WIDTH + 2 * STATE), F32),
            pltpu.VMEM((HEADS, TOKENS), F32),
            pltpu.VMEM((2 + BITS, HEADS, TOKENS), F32),
            pltpu.VMEM((1, WIDTH), F32),
            pltpu.VMEM((16, WIDTH + 2 * STATE), BF16),
            pltpu.VMEM((PIECES, 2, WIDTH, HALF), BF16),
            pltpu.VMEM((PIECES, STRETCH, STATE), BF16),
            pltpu.VMEM((PIECES, 2, STATE, HALF), BF16),
            pltpu.VMEM((PIECES, HEADS, STRETCH), F32),
            pltpu.VMEM((PIECES, STRETCH, HEADS), F32),
            pltpu.VMEM((PIECES, WIDTH, STATE), F32),
            pltpu.VMEM((PIECES - 1, WIDTH, STATE), BF16),
            pltpu.VMEM((PIECES, 2, WIDTH, HALF), F32),
            pltpu.VMEM((WIDTH, 1), F32),
            pltpu.VMEM((TOKENS // HALF, BITS, HEADS, HALF), F32),
            pltpu.VMEM((GROUP, ROWS, STATE), BF16),
            pltpu.VMEM((GROUP, ROWS, STATE), BF16),
            pltpu.VMEM((SHARDS, HEADS, HALF), F32),
            pltpu.VMEM((MIDDLE, GROUP, ROWS, STATE), BF16),
            pltpu.VMEM((ROWS, STATE), BF16),
            pltpu.VMEM((BITS, GROUP, ROWS, STATE), BF16),
            pltpu.SemaphoreType.DMA((4,)),
            pltpu.SemaphoreType.DMA((PIECES + 1,)),
            pltpu.SemaphoreType.DMA((TOKENS // HALF,)),
            pltpu.SemaphoreType.DMA((2,)),
            pltpu.SemaphoreType.DMA,
            pltpu.SemaphoreType.DMA,
            pltpu.SemaphoreType.DMA((4,)),
            pltpu.SemaphoreType.DMA((2,)),
            pltpu.SemaphoreType.DMA((2,)),
            pltpu.SemaphoreType.DMA,
            pltpu.SemaphoreType.DMA,
        ],
        compiler_params=pltpu.CompilerParams(
            collective_id=0, has_side_effects=True, vmem_limit_bytes=63 << 20
        ),
    )(mixer_input, conv_weight, log_decay, level_weight, norm_gain.reshape(1, WIDTH))
    return blocks.transpose(0, 2, 1).reshape(TOKENS, WIDTH)


def solution(mesh):
    placed = (
        P("ctx", "heads"),
        P(None, "heads"),
        P("heads", "ctx"),
        P(None, "heads", "ctx"),
        P("heads"),
    )
    return jax.shard_map(
        per_device, mesh=mesh, in_specs=placed, out_specs=P("ctx", "heads"), check_vma=False
    )
```

```python
import functools

import jax
import jax.numpy as jnp
from jax import lax
from jax.experimental import pallas as pl
from jax.experimental.pallas import tpu as pltpu
from jax.sharding import PartitionSpec as P

HEADS = 8
HEAD_DIM = 64
STATE = 128
STRETCH = 256
WIDTH = 512
TOKENS = 1024
PIECES = TOKENS // STRETCH
SHARDS = 32
ALONG_Z = 8
ALONG_Y = 4
OFFSETS = (4, 3, 5, 2, 6, 1, 7, 0)
BITS = 5
HALF = 128
GROUP = 16
ROWS = WIDTH // GROUP
MIDDLE = 3
LOG2E = 1.4426950408889634

NT = (((1,), (1,)), ((), ()))
F32 = jnp.float32
BF16 = jnp.bfloat16


def popcount(r):
    count = r % 2
    for k in range(1, BITS):
        count = count + (r // 2**k) % 2
    return count


def activate(window, conv_ref, cols):
    total = conv_ref[3:4, cols] * window[16:144]
    for j in range(3):
        total = total + conv_ref[j : j + 1, cols] * window[13 + j : 141 + j]
    half = 0.5 * total
    return (half + half * jnp.tanh(half)).astype(BF16)


def kernel(
    x_hbm, conv_hbm, rate_hbm, level_hbm, gain_hbm, out_hbm,
    out_ref, x_ref, conv_ref, rate_ref, level_ref, gain_ref, halo, xt, keys, qt, inner, column, state, low, mixed, gain_col, slot_weight,
    send1, recv1, spans, stage, top, recv3,
    in_sem, x_sem, out_sem, halo_sem, p1_send, p1_recv, span_sem, p0_sem, p4_sem, p3_send, p3_recv,
):
    me = lax.axis_index("ctx")
    bits = popcount(me)
    pair = me // GROUP
    place_in = lax.rem(me, GROUP)
    odd = lax.rem(me, 2)
    place_z = lax.rem(me, ALONG_Z)
    row_in = place_in // ALONG_Z
    middle = popcount(place_in // 2)

    barrier = pltpu.get_barrier_semaphore()

    small_in = [
        pltpu.make_async_copy(src, dst, in_sem.at[i])
        for i, (src, dst) in enumerate(
            ((rate_hbm, rate_ref), (conv_hbm, conv_ref), (gain_hbm, gain_ref), (level_hbm, level_ref))
        )
    ]

    def rows_in(start, count, at):
        span_of = pl.ds(start, count)
        return pltpu.make_async_copy(x_hbm.at[span_of], x_ref.at[span_of], x_sem.at[at])

    def stretch_in(c):
        return rows_in(pl.multiple_of(c * STRETCH - 16, 16), STRETCH, c)

    head_in = rows_in(0, STRETCH - 16, 0)
    tail_in = rows_in(TOKENS - 16, 16, PIECES)
    small_in[0].start()
    tail_in.start()
    stretch_in(PIECES - 1).start()

    def greet(d, _):
        other = lax.rem(me + d, SHARDS)
        pl.semaphore_signal(barrier, inc=1, device_id={"ctx": other})
        return 0

    lax.fori_loop(1, SHARDS, greet, 0)

    small_in[1].start()
    small_in[2].start()
    for c in range(PIECES - 2, 0, -1):
        stretch_in(c).start()
    head_in.start()
    small_in[3].start()

    small_in[0].wait()
    rows = lax.broadcasted_iota(jnp.int32, (STRETCH, STRETCH), 0)
    cols = lax.broadcasted_iota(jnp.int32, (STRETCH, STRETCH), 1)
    lower = jnp.where(rows >= cols, 1.0, 0.0).astype(F32)
    rates = jnp.concatenate(
        [rate_ref[:, c * STRETCH : (c + 1) * STRETCH] for c in range(PIECES)], axis=0
    )
    sums = lax.dot_general(
        rates * LOG2E, lower, NT, precision=lax.Precision.HIGHEST, preferred_element_type=F32
    )
    span = jnp.zeros((HEADS, HALF), F32)
    for c in range(PIECES):
        part = sums[c * HEADS : (c + 1) * HEADS]
        inner[c] = part
        span = span + jnp.broadcast_to(part[:, STRETCH - 1 :], (HEADS, HALF))
    spans[me] = span
    small_in[1].wait()

    row_start = me - lax.rem(me, ALONG_Z)

    def to_row(d):
        return row_start + lax.rem(me + d, ALONG_Z)

    def to_column(d):
        return lax.rem(me + d * ALONG_Z, SHARDS)

    def span_along_row(d):
        return pltpu.make_async_remote_copy(
            src_ref=spans.at[me], dst_ref=spans.at[me],
            send_sem=span_sem.at[0], recv_sem=span_sem.at[1], device_id={"ctx": to_row(d)},
        )

    def span_along_column(d):
        at = pl.ds(row_start, ALONG_Z)
        return pltpu.make_async_remote_copy(
            src_ref=spans.at[at], dst_ref=spans.at[at],
            send_sem=span_sem.at[2], recv_sem=span_sem.at[3], device_id={"ctx": to_column(d)},
        )

    def wait_bytes(ref, count, send_sem, recv_sem):
        part = ref.at[pl.ds(0, count)]
        return pltpu.make_async_remote_copy(
            src_ref=part, dst_ref=part, send_sem=send_sem, recv_sem=recv_sem,
            device_id={"ctx": lax.rem(me + 1, SHARDS)},
        )

    to_next = pltpu.make_async_remote_copy(
        src_ref=x_ref.at[pl.ds(TOKENS - 16, 16)], dst_ref=halo,
        send_sem=halo_sem.at[0], recv_sem=halo_sem.at[1],
        device_id={"ctx": lax.rem(me + 1, SHARDS)},
    )

    def place(b, group, act):
        c, half = b // 2, b % 2
        if group < 4:
            xt[c, half, group * HALF : (group + 1) * HALF] = act.T
        elif group == 4:
            keys[c, pl.ds(pl.multiple_of(half * HALF, HALF), HALF)] = act
        else:
            qt[c, half] = act.T

    def block(b):
        start = pl.multiple_of(b * HALF - 16, 16)
        for group in range(6):
            chans = slice(group * HALF, (group + 1) * HALF)
            window = x_ref[pl.ds(start, HALF + 16), chans].astype(F32)
            place(b, group, activate(window, conv_ref, chans))

    def stretch_state(c):
        to_end = jnp.exp2(inner[c, :, STRETCH - 1 :] - inner[c])
        parts = []
        for h in range(HEADS):
            x_h = jnp.concatenate(
                [xt[c, 0, h * HEAD_DIM : (h + 1) * HEAD_DIM], xt[c, 1, h * HEAD_DIM : (h + 1) * HEAD_DIM]],
                axis=1,
            )
            parts.append((x_h.astype(F32) * to_end[h : h + 1]).astype(BF16))
        state[c] = jnp.dot(
            jnp.concatenate(parts, axis=0), keys[c], preferred_element_type=F32
        )

    tail_in.wait()

    def late(i, _):
        c = PIECES - 1 - i
        stretch_in(c).wait()
        lax.fori_loop(0, 2, lambda half, _: (block(2 * c + 1 - half), 0)[1], 0)
        stretch_state(c)

        @pl.when(i == 0)
        def _():
            pl.semaphore_wait(barrier, SHARDS - 1)

            @pl.when(me < SHARDS - 1)
            def _():
                to_next.start()

            for d in range(1, ALONG_Z):
                span_along_row(d).start()

        return 0

    lax.fori_loop(0, PIECES - 1, late, 0)
    head_in.wait()
    block(1)

    @pl.when(me == 0)
    def _():
        halo[...] = jnp.zeros_like(halo)

    @pl.when(me > 0)
    def _():
        to_next.wait_recv()


    for group in range(6):
        chans = slice(group * HALF, (group + 1) * HALF)
        window = jnp.concatenate([halo[:, chans], x_ref[:HALF, chans]], axis=0).astype(F32)
        place(0, group, activate(window, conv_ref, chans))
    stretch_state(0)

    for h in range(HEADS):
        at = slice(h * HEAD_DIM, (h + 1) * HEAD_DIM)
        carried = state[0, at]
        for c in range(1, PIECES):
            low[c - 1, at] = carried.astype(BF16)
            fall = jnp.exp2(
                jnp.broadcast_to(inner[c, h : h + 1, STRETCH - 1 :], (1, STATE))
            )
            carried = fall * carried + state[c, at]
        send1[2 * h : 2 * (h + 1)] = carried.astype(BF16).reshape(2, ROWS, STATE)

    def across(along, down):
        return (row_in + down) % 2 * ALONG_Z + lax.rem(place_z + along, ALONG_Z)

    for along in OFFSETS:
        for down in (1, 0):
            if along or down:
                there = across(along, down)
                pltpu.make_async_remote_copy(
                    src_ref=send1.at[there], dst_ref=recv1.at[place_in],
                    send_sem=p1_send, recv_sem=p1_recv, device_id={"ctx": pair * GROUP + there},
                ).start()

    recv1[place_in] = send1[place_in]

    small_in[2].wait()
    diag = (rows == cols)[:HALF, :HALF]
    for g in range(WIDTH // HALF):
        row = jnp.broadcast_to(gain_ref[:, g * HALF : (g + 1) * HALF], (HALF, HALF))
        gain_col[g * HALF : (g + 1) * HALF] = jnp.sum(
            jnp.where(diag, row, 0.0), axis=1, keepdims=True
        )
    for c in range(PIECES):
        rate = rate_ref[:, c * STRETCH : (c + 1) * STRETCH] * LOG2E
        column[c] = lax.dot_general(
            lower, rate, NT, precision=lax.Precision.HIGHEST, preferred_element_type=F32
        )
    causal = (rows <= cols)[:HALF, :HALF]

    def near_own(c, before):
        q = [qt[c, 0], qt[c, 1]]
        k = keys[c]
        for half in range(2):
            width = HALF * (half + 1)
            score = jnp.dot(k[:width], q[half], preferred_element_type=F32)
            at_t = pl.ds(pl.multiple_of(c * STRETCH, STRETCH) + half * HALF, HALF)
            row_all = inner[c, :, half * HALF : (half + 1) * HALF]
            own_scale = level_ref[0, :, at_t]
            near_scale = level_ref[1, :, at_t] * jnp.exp2(row_all)
            if before:
                readout = jnp.dot(low[c - 1], q[half], preferred_element_type=F32)
            for h in range(HEADS):
                at = slice(h * HEAD_DIM, (h + 1) * HEAD_DIM)
                gap = row_all[h : h + 1] - column[c, :width, h : h + 1]
                blocks = []
                if half == 1:
                    blocks.append((jnp.exp2(gap[:HALF]) * score[:HALF]).astype(BF16))
                last = jnp.where(causal, gap[width - HALF :], -jnp.inf)
                blocks.append((jnp.exp2(last) * score[width - HALF :]).astype(BF16))
                own = jnp.dot(xt[c, half, at], blocks[-1], preferred_element_type=F32)
                if half == 1:
                    own = own + jnp.dot(xt[c, 0, at], blocks[0], preferred_element_type=F32)
                own = own * own_scale[h : h + 1]
                if before:
                    own = own + readout[at] * near_scale[h : h + 1]
                mixed[c, half, at] = own

    neighbour = pltpu.make_async_remote_copy(
        src_ref=send1, dst_ref=recv3.at[pair],
        send_sem=p0_sem.at[0], recv_sem=p0_sem.at[1],
        device_id={"ctx": lax.rem(me + 1, SHARDS)},
    )

    @pl.when(odd == 0)
    def _():
        neighbour.start()

    small_in[3].wait()
    near_own(0, False)
    wait_bytes(spans, ALONG_Z - 1, span_sem.at[0], span_sem.at[1]).wait()
    for d in range(1, ALONG_Y):
        span_along_column(d).start()

    def rest(c, _):
        near_own(c, True)

        return 0

    lax.fori_loop(1, PIECES, rest, 0)

    wait_bytes(recv1, GROUP - 1, p1_send, p1_recv).wait()
    wait_bytes(spans, SHARDS - ALONG_Z, span_sem.at[2], span_sem.at[3]).wait()
    head = place_in // (GROUP // HEADS)
    ends = [recv1[q].astype(F32) for q in range(GROUP)]
    falls = [spans[pair * GROUP + q, pl.ds(head, 1)] for q in range(GROUP)]
    for k in range(BITS - 1):
        if k > 0:
            for group in range(0, len(ends), 2):
                left = ends[group].astype(BF16)
                for r in range((group + 1) << k, (group + 2) << k):
                    stage[popcount((r // 2) % 2 ** (k - 1)), r] = left
        ends = [
            jnp.exp2(falls[i + 1]) * ends[i] + ends[i + 1] for i in range(0, len(ends), 2)
        ]
        falls = [falls[i] + falls[i + 1] for i in range(0, len(falls), 2)]
    top[...] = ends[0].astype(BF16)

    def answer(there):
        @pl.when(pair == 0)
        def _():
            pltpu.make_async_remote_copy(
                src_ref=top, dst_ref=recv3.at[0, place_in],
                send_sem=p4_sem.at[0], recv_sem=p4_sem.at[1],
                device_id={"ctx": GROUP + there},
            ).start()

        count = popcount(there // 2) * jnp.where(there == place_in, 0, 1)
        for n in range(1, MIDDLE + 1):

            @pl.when(count == n)
            def _():
                pltpu.make_async_remote_copy(
                    src_ref=stage.at[pl.ds(0, n), there],
                    dst_ref=recv3.at[pl.ds(pair + lax.rem(there, 2), n), place_in],
                    send_sem=p3_send, recv_sem=p3_recv,
                    device_id={"ctx": pair * GROUP + there},
                ).start()


    for t in range(4):
        turn = lax.rem(place_in + t, 4)
        answer(turn // 2 * ALONG_Z + turn % 2)
    for along in OFFSETS:
        for down in (1, 0):
            there = across(along, down)

            @pl.when(lax.rem(there, ALONG_Z) >= 2)
            def _(there=there):
                answer(there)

    for n in range(1, MIDDLE + 1):

        @pl.when(middle == n)
        def _():
            recv3[pl.ds(pair + odd, n), place_in] = stage[:n, place_in]

    for k in range(BITS):
        digit = (me // 2**k) % 2
        if k == 0:
            slot = pair
        elif k == BITS - 1:
            slot = 0
        else:
            slot = pair + odd + popcount((me // 2) % 2 ** (k - 1))
        first = (me // 2**k) * 2**k

        @pl.when(digit == 1)
        def _():
            def add(q, total):
                return total + spans[q]

            between = lax.fori_loop(first, me, add, jnp.zeros((HEADS, HALF), F32))
            for c in range(PIECES):
                gap = between + jnp.zeros((HEADS, HALF), F32)
                for e in range(c):
                    gap = gap + jnp.broadcast_to(inner[e, :, STRETCH - 1 :], (HEADS, HALF))
                for half in range(2):
                    tokens = slice((2 * c + half) * HALF, (2 * c + half + 1) * HALF)
                    slot_weight[2 * c + half, slot] = level_ref[2 + k, :, tokens] * jnp.exp2(
                        gap + inner[c, :, half * HALF : (half + 1) * HALF]
                    )

    def add_bucket(i, _):
        slot = lax.rem(pair + i, bits)

        @pl.when((odd == 1) & (i == 0))
        def _():
            neighbour.wait_recv()

        for n in range(1, MIDDLE + 1):

            @pl.when((middle == n) & (i == odd))
            def _():
                part = recv3.at[pl.ds(0, n), pl.ds(0, GROUP - 1)]
                pltpu.make_async_remote_copy(
                    src_ref=part, dst_ref=part, send_sem=p3_send, recv_sem=p3_recv,
                    device_id={"ctx": lax.rem(me + 1, SHARDS)},
                ).wait_recv()

        @pl.when((pair == 1) & (i == bits - 1))
        def _():
            wait_bytes(recv1, GROUP, p4_sem.at[0], p4_sem.at[1]).wait_recv()

        for c in range(PIECES):
            q = jnp.concatenate([qt[c, 0], qt[c, 1]], axis=1)
            for g in range(4):
                bucket = recv3[slot, g * 4 : (g + 1) * 4].reshape(HALF, STATE)
                readout = jnp.dot(bucket, q, preferred_element_type=F32)
                for half in range(2):
                    lanes = slice(half * HALF, (half + 1) * HALF)
                    for h in range(2):
                        at = slice(h * HEAD_DIM, (h + 1) * HEAD_DIM)
                        to = slice(g * HALF + h * HEAD_DIM, g * HALF + (h + 1) * HEAD_DIM)
                        weight = slot_weight[2 * c + half, slot, 2 * g + h : 2 * g + h + 1]
                        mixed[c, half, to] = mixed[c, half, to] + readout[at, lanes] * weight
        return 0

    lax.fori_loop(0, bits, add_bucket, 0)

    def tokens_out(b):
        return pltpu.make_async_copy(out_ref.at[b], out_hbm.at[b], out_sem.at[b])

    for b in range(TOKENS // HALF):
        c, half = b // 2, b % 2
        square = jnp.zeros((HEAD_DIM, HALF), F32)
        for h in range(HEADS):
            part = mixed[c, half, h * HEAD_DIM : (h + 1) * HEAD_DIM]
            square = square + part * part
        mean = jnp.sum(square, axis=0, keepdims=True) * (1.0 / WIDTH)
        scale = lax.rsqrt(mean + 1e-05)
        out_ref[b] = (mixed[c, half] * scale * gain_col[...]).astype(BF16)
        tokens_out(b).start()

    @pl.when(me < SHARDS - 1)
    def _():
        to_next.wait_send()

    @pl.when(odd == 0)
    def _():
        neighbour.wait_send()

    @pl.when(pair == 0)
    def _():
        wait_bytes(recv1, GROUP, p4_sem.at[0], p4_sem.at[1]).wait_send()

    for n in range(MIDDLE + 1):

        @pl.when(middle == n)
        def _():
            for part in (stage.at[0], stage.at[1, pl.ds(0, GROUP // 2 - n)]):
                pltpu.make_async_remote_copy(
                    src_ref=part, dst_ref=part, send_sem=p3_send, recv_sem=p3_recv,
                    device_id={"ctx": lax.rem(me + 1, SHARDS)},
                ).wait_send()

    for b in range(TOKENS // HALF):
        tokens_out(b).wait()


def per_device(mixer_input, conv_weight, log_decay, level_weight, norm_gain):
    hbm = pl.BlockSpec(memory_space=pltpu.HBM)
    blocks = pl.pallas_call(
        kernel,
        out_shape=jax.ShapeDtypeStruct((TOKENS // HALF, WIDTH, HALF), BF16),
        in_specs=[hbm] * 5,
        out_specs=hbm,
        scratch_shapes=[
            pltpu.VMEM((TOKENS // HALF, WIDTH, HALF), BF16),
            pltpu.VMEM((TOKENS, WIDTH + 2 * STATE), BF16),
            pltpu.VMEM((4, WIDTH + 2 * STATE), F32),
            pltpu.VMEM((HEADS, TOKENS), F32),
            pltpu.VMEM((2 + BITS, HEADS, TOKENS), F32),
            pltpu.VMEM((1, WIDTH), F32),
            pltpu.VMEM((16, WIDTH + 2 * STATE), BF16),
            pltpu.VMEM((PIECES, 2, WIDTH, HALF), BF16),
            pltpu.VMEM((PIECES, STRETCH, STATE), BF16),
            pltpu.VMEM((PIECES, 2, STATE, HALF), BF16),
            pltpu.VMEM((PIECES, HEADS, STRETCH), F32),
            pltpu.VMEM((PIECES, STRETCH, HEADS), F32),
            pltpu.VMEM((PIECES, WIDTH, STATE), F32),
            pltpu.VMEM((PIECES - 1, WIDTH, STATE), BF16),
            pltpu.VMEM((PIECES, 2, WIDTH, HALF), F32),
            pltpu.VMEM((WIDTH, 1), F32),
            pltpu.VMEM((TOKENS // HALF, BITS, HEADS, HALF), F32),
            pltpu.VMEM((GROUP, ROWS, STATE), BF16),
            pltpu.VMEM((GROUP, ROWS, STATE), BF16),
            pltpu.VMEM((SHARDS, HEADS, HALF), F32),
            pltpu.VMEM((MIDDLE, GROUP, ROWS, STATE), BF16),
            pltpu.VMEM((ROWS, STATE), BF16),
            pltpu.VMEM((BITS, GROUP, ROWS, STATE), BF16),
            pltpu.SemaphoreType.DMA((4,)),
            pltpu.SemaphoreType.DMA((PIECES + 1,)),
            pltpu.SemaphoreType.DMA((TOKENS // HALF,)),
            pltpu.SemaphoreType.DMA((2,)),
            pltpu.SemaphoreType.DMA,
            pltpu.SemaphoreType.DMA,
            pltpu.SemaphoreType.DMA((4,)),
            pltpu.SemaphoreType.DMA((2,)),
            pltpu.SemaphoreType.DMA((2,)),
            pltpu.SemaphoreType.DMA,
            pltpu.SemaphoreType.DMA,
        ],
        compiler_params=pltpu.CompilerParams(
            collective_id=0, has_side_effects=True, vmem_limit_bytes=63 << 20
        ),
    )(mixer_input, conv_weight, log_decay, level_weight, norm_gain.reshape(1, WIDTH))
    return blocks.transpose(0, 2, 1).reshape(TOKENS, WIDTH)


def solution(mesh):
    placed = (
        P("ctx", "heads"),
        P(None, "heads"),
        P("heads", "ctx"),
        P(None, "heads", "ctx"),
        P("heads"),
    )
    return jax.shard_map(
        per_device, mesh=mesh, in_specs=placed, out_specs=P("ctx", "heads"), check_vma=False
    )
```

```python
import functools

import jax
import jax.numpy as jnp
from jax import lax
from jax.experimental import pallas as pl
from jax.experimental.pallas import tpu as pltpu
from jax.sharding import PartitionSpec as P

HEADS = 8
HEAD_DIM = 64
STATE = 128
STRETCH = 256
WIDTH = 512
TOKENS = 1024
PIECES = TOKENS // STRETCH
SHARDS = 32
ALONG_Z = 8
ALONG_Y = 4
OFFSETS = (4, 3, 5, 2, 6, 1, 7, 0)
ANSWERS = (5, 6, 7, 4, 3, 2, 1, 0)
BITS = 5
HALF = 128
GROUP = 16
ROWS = WIDTH // GROUP
MIDDLE = 3
LOG2E = 1.4426950408889634

NT = (((1,), (1,)), ((), ()))
F32 = jnp.float32
BF16 = jnp.bfloat16


def popcount(r):
    count = r % 2
    for k in range(1, BITS):
        count = count + (r // 2**k) % 2
    return count


def activate(window, conv_ref, cols):
    total = conv_ref[3:4, cols] * window[16:144]
    for j in range(3):
        total = total + conv_ref[j : j + 1, cols] * window[13 + j : 141 + j]
    half = 0.5 * total
    return (half + half * jnp.tanh(half)).astype(BF16)


def kernel(
    x_hbm, conv_hbm, rate_hbm, level_hbm, gain_hbm, out_hbm,
    out_ref, x_ref, conv_ref, rate_ref, level_ref, gain_ref, halo, xt, keys, qt, inner, column, state, low, mixed, gain_col, slot_weight,
    send1, recv1, spans, stage, top, recv3,
    in_sem, x_sem, out_sem, halo_sem, p1_send, p1_recv, span_sem, p0_sem, p4_sem, p3_send, p3_recv,
):
    me = lax.axis_index("ctx")
    bits = popcount(me)
    pair = me // GROUP
    place_in = lax.rem(me, GROUP)
    odd = lax.rem(me, 2)
    place_z = lax.rem(me, ALONG_Z)
    row_in = place_in // ALONG_Z
    middle = popcount(place_in // 2)

    barrier = pltpu.get_barrier_semaphore()

    small_in = [
        pltpu.make_async_copy(src, dst, in_sem.at[i])
        for i, (src, dst) in enumerate(
            ((rate_hbm, rate_ref), (conv_hbm, conv_ref), (gain_hbm, gain_ref), (level_hbm, level_ref))
        )
    ]

    def rows_in(start, count, at):
        span_of = pl.ds(start, count)
        return pltpu.make_async_copy(x_hbm.at[span_of], x_ref.at[span_of], x_sem.at[at])

    def stretch_in(c):
        return rows_in(pl.multiple_of(c * STRETCH - 16, 16), STRETCH, c)

    head_in = rows_in(0, STRETCH - 16, 0)
    tail_in = rows_in(TOKENS - 16, 16, PIECES)
    small_in[0].start()
    tail_in.start()
    stretch_in(PIECES - 1).start()

    def greet(d, _):
        other = lax.rem(me + d, SHARDS)
        pl.semaphore_signal(barrier, inc=1, device_id={"ctx": other})
        return 0

    lax.fori_loop(1, SHARDS, greet, 0)

    small_in[1].start()
    small_in[2].start()
    for c in range(PIECES - 2, 0, -1):
        stretch_in(c).start()
    head_in.start()
    small_in[3].start()

    small_in[0].wait()
    rows = lax.broadcasted_iota(jnp.int32, (STRETCH, STRETCH), 0)
    cols = lax.broadcasted_iota(jnp.int32, (STRETCH, STRETCH), 1)
    lower = jnp.where(rows >= cols, 1.0, 0.0).astype(F32)
    rates = jnp.concatenate(
        [rate_ref[:, c * STRETCH : (c + 1) * STRETCH] for c in range(PIECES)], axis=0
    )
    sums = lax.dot_general(
        rates * LOG2E, lower, NT, precision=lax.Precision.HIGHEST, preferred_element_type=F32
    )
    span = jnp.zeros((HEADS, HALF), F32)
    for c in range(PIECES):
        part = sums[c * HEADS : (c + 1) * HEADS]
        inner[c] = part
        span = span + jnp.broadcast_to(part[:, STRETCH - 1 :], (HEADS, HALF))
    spans[me] = span
    small_in[1].wait()

    row_start = me - lax.rem(me, ALONG_Z)

    def to_row(d):
        return row_start + lax.rem(me + d, ALONG_Z)

    def to_column(d):
        return lax.rem(me + d * ALONG_Z, SHARDS)

    def span_along_row(d):
        return pltpu.make_async_remote_copy(
            src_ref=spans.at[me], dst_ref=spans.at[me],
            send_sem=span_sem.at[0], recv_sem=span_sem.at[1], device_id={"ctx": to_row(d)},
        )

    def span_along_column(d):
        at = pl.ds(row_start, ALONG_Z)
        return pltpu.make_async_remote_copy(
            src_ref=spans.at[at], dst_ref=spans.at[at],
            send_sem=span_sem.at[2], recv_sem=span_sem.at[3], device_id={"ctx": to_column(d)},
        )

    def wait_bytes(ref, count, send_sem, recv_sem):
        part = ref.at[pl.ds(0, count)]
        return pltpu.make_async_remote_copy(
            src_ref=part, dst_ref=part, send_sem=send_sem, recv_sem=recv_sem,
            device_id={"ctx": lax.rem(me + 1, SHARDS)},
        )

    to_next = pltpu.make_async_remote_copy(
        src_ref=x_ref.at[pl.ds(TOKENS - 16, 16)], dst_ref=halo,
        send_sem=halo_sem.at[0], recv_sem=halo_sem.at[1],
        device_id={"ctx": lax.rem(me + 1, SHARDS)},
    )

    def place(b, group, act):
        c, half = b // 2, b % 2
        if group < 4:
            xt[c, half, group * HALF : (group + 1) * HALF] = act.T
        elif group == 4:
            keys[c, pl.ds(pl.multiple_of(half * HALF, HALF), HALF)] = act
        else:
            qt[c, half] = act.T

    def block(b):
        start = pl.multiple_of(b * HALF - 16, 16)
        for group in range(6):
            chans = slice(group * HALF, (group + 1) * HALF)
            window = x_ref[pl.ds(start, HALF + 16), chans].astype(F32)
            place(b, group, activate(window, conv_ref, chans))

    def stretch_state(c):
        to_end = jnp.exp2(inner[c, :, STRETCH - 1 :] - inner[c])
        parts = []
        for h in range(HEADS):
            x_h = jnp.concatenate(
                [xt[c, 0, h * HEAD_DIM : (h + 1) * HEAD_DIM], xt[c, 1, h * HEAD_DIM : (h + 1) * HEAD_DIM]],
                axis=1,
            )
            parts.append((x_h.astype(F32) * to_end[h : h + 1]).astype(BF16))
        state[c] = jnp.dot(
            jnp.concatenate(parts, axis=0), keys[c], preferred_element_type=F32
        )

    tail_in.wait()

    def late(i, _):
        c = PIECES - 1 - i
        stretch_in(c).wait()
        lax.fori_loop(0, 2, lambda half, _: (block(2 * c + 1 - half), 0)[1], 0)
        stretch_state(c)

        @pl.when(i == 0)
        def _():
            pl.semaphore_wait(barrier, SHARDS - 1)

            @pl.when(me < SHARDS - 1)
            def _():
                to_next.start()

            for d in range(1, ALONG_Z):
                span_along_row(d).start()

        return 0

    lax.fori_loop(0, PIECES - 1, late, 0)
    head_in.wait()
    block(1)

    @pl.when(me == 0)
    def _():
        halo[...] = jnp.zeros_like(halo)

    @pl.when(me > 0)
    def _():
        to_next.wait_recv()


    for group in range(6):
        chans = slice(group * HALF, (group + 1) * HALF)
        window = jnp.concatenate([halo[:, chans], x_ref[:HALF, chans]], axis=0).astype(F32)
        place(0, group, activate(window, conv_ref, chans))
    stretch_state(0)

    for h in range(HEADS):
        at = slice(h * HEAD_DIM, (h + 1) * HEAD_DIM)
        carried = state[0, at]
        for c in range(1, PIECES):
            low[c - 1, at] = carried.astype(BF16)
            fall = jnp.exp2(
                jnp.broadcast_to(inner[c, h : h + 1, STRETCH - 1 :], (1, STATE))
            )
            carried = fall * carried + state[c, at]
        send1[2 * h : 2 * (h + 1)] = carried.astype(BF16).reshape(2, ROWS, STATE)

    def across(along, down):
        return (row_in + down) % 2 * ALONG_Z + lax.rem(place_z + along, ALONG_Z)

    for along in OFFSETS:
        for down in (0, 1):
            if along or down:
                there = across(along, down)
                pltpu.make_async_remote_copy(
                    src_ref=send1.at[there], dst_ref=recv1.at[place_in],
                    send_sem=p1_send, recv_sem=p1_recv, device_id={"ctx": pair * GROUP + there},
                ).start()

    recv1[place_in] = send1[place_in]

    small_in[2].wait()
    diag = (rows == cols)[:HALF, :HALF]
    for g in range(WIDTH // HALF):
        row = jnp.broadcast_to(gain_ref[:, g * HALF : (g + 1) * HALF], (HALF, HALF))
        gain_col[g * HALF : (g + 1) * HALF] = jnp.sum(
            jnp.where(diag, row, 0.0), axis=1, keepdims=True
        )
    for c in range(PIECES):
        rate = rate_ref[:, c * STRETCH : (c + 1) * STRETCH] * LOG2E
        column[c] = lax.dot_general(
            lower, rate, NT, precision=lax.Precision.HIGHEST, preferred_element_type=F32
        )
    causal = (rows <= cols)[:HALF, :HALF]

    def near_own(c, before):
        q = [qt[c, 0], qt[c, 1]]
        k = keys[c]
        for half in range(2):
            width = HALF * (half + 1)
            score = jnp.dot(k[:width], q[half], preferred_element_type=F32)
            at_t = pl.ds(pl.multiple_of(c * STRETCH, STRETCH) + half * HALF, HALF)
            row_all = inner[c, :, half * HALF : (half + 1) * HALF]
            own_scale = level_ref[0, :, at_t]
            near_scale = level_ref[1, :, at_t] * jnp.exp2(row_all)
            if before:
                readout = jnp.dot(low[c - 1], q[half], preferred_element_type=F32)
            for h in range(HEADS):
                at = slice(h * HEAD_DIM, (h + 1) * HEAD_DIM)
                gap = row_all[h : h + 1] - column[c, :width, h : h + 1]
                blocks = []
                if half == 1:
                    blocks.append((jnp.exp2(gap[:HALF]) * score[:HALF]).astype(BF16))
                last = jnp.where(causal, gap[width - HALF :], -jnp.inf)
                blocks.append((jnp.exp2(last) * score[width - HALF :]).astype(BF16))
                own = jnp.dot(xt[c, half, at], blocks[-1], preferred_element_type=F32)
                if half == 1:
                    own = own + jnp.dot(xt[c, 0, at], blocks[0], preferred_element_type=F32)
                own = own * own_scale[h : h + 1]
                if before:
                    own = own + readout[at] * near_scale[h : h + 1]
                mixed[c, half, at] = own

    neighbour = pltpu.make_async_remote_copy(
        src_ref=send1, dst_ref=recv3.at[pair],
        send_sem=p0_sem.at[0], recv_sem=p0_sem.at[1],
        device_id={"ctx": lax.rem(me + 1, SHARDS)},
    )

    @pl.when(odd == 0)
    def _():
        neighbour.start()

    small_in[3].wait()
    near_own(0, False)
    wait_bytes(spans, ALONG_Z - 1, span_sem.at[0], span_sem.at[1]).wait()
    for d in range(1, ALONG_Y):
        span_along_column(d).start()

    def rest(c, _):
        near_own(c, True)

        return 0

    lax.fori_loop(1, PIECES, rest, 0)

    wait_bytes(recv1, GROUP - 1, p1_send, p1_recv).wait()
    wait_bytes(spans, SHARDS - ALONG_Z, span_sem.at[2], span_sem.at[3]).wait()
    head = place_in // (GROUP // HEADS)
    ends = [recv1[q].astype(F32) for q in range(GROUP)]
    falls = [spans[pair * GROUP + q, pl.ds(head, 1)] for q in range(GROUP)]
    for k in range(BITS - 1):
        if k > 0:
            for group in range(0, len(ends), 2):
                left = ends[group].astype(BF16)
                for r in range((group + 1) << k, (group + 2) << k):
                    stage[popcount((r // 2) % 2 ** (k - 1)), r] = left
        ends = [
            jnp.exp2(falls[i + 1]) * ends[i] + ends[i + 1] for i in range(0, len(ends), 2)
        ]
        falls = [falls[i] + falls[i + 1] for i in range(0, len(falls), 2)]
    top[...] = ends[0].astype(BF16)

    def answer(there):
        @pl.when(pair == 0)
        def _():
            pltpu.make_async_remote_copy(
                src_ref=top, dst_ref=recv3.at[0, place_in],
                send_sem=p4_sem.at[0], recv_sem=p4_sem.at[1],
                device_id={"ctx": GROUP + there},
            ).start()

        count = popcount(there // 2) * jnp.where(there == place_in, 0, 1)
        for n in range(1, MIDDLE + 1):

            @pl.when(count == n)
            def _():
                pltpu.make_async_remote_copy(
                    src_ref=stage.at[pl.ds(0, n), there],
                    dst_ref=recv3.at[pl.ds(pair + lax.rem(there, 2), n), place_in],
                    send_sem=p3_send, recv_sem=p3_recv,
                    device_id={"ctx": pair * GROUP + there},
                ).start()


    for t in range(4):
        turn = lax.rem(place_in + t, 4)
        answer(turn // 2 * ALONG_Z + turn % 2)
    for along in ANSWERS:
        for down in (1, 0):
            there = across(along, down)

            @pl.when(lax.rem(there, ALONG_Z) >= 2)
            def _(there=there):
                answer(there)

    for n in range(1, MIDDLE + 1):

        @pl.when(middle == n)
        def _():
            recv3[pl.ds(pair + odd, n), place_in] = stage[:n, place_in]

    for k in range(BITS):
        digit = (me // 2**k) % 2
        if k == 0:
            slot = pair
        elif k == BITS - 1:
            slot = 0
        else:
            slot = pair + odd + popcount((me // 2) % 2 ** (k - 1))
        first = (me // 2**k) * 2**k

        @pl.when(digit == 1)
        def _():
            def add(q, total):
                return total + spans[q]

            between = lax.fori_loop(first, me, add, jnp.zeros((HEADS, HALF), F32))
            for c in range(PIECES):
                gap = between + jnp.zeros((HEADS, HALF), F32)
                for e in range(c):
                    gap = gap + jnp.broadcast_to(inner[e, :, STRETCH - 1 :], (HEADS, HALF))
                for half in range(2):
                    tokens = slice((2 * c + half) * HALF, (2 * c + half + 1) * HALF)
                    slot_weight[2 * c + half, slot] = level_ref[2 + k, :, tokens] * jnp.exp2(
                        gap + inner[c, :, half * HALF : (half + 1) * HALF]
                    )

    def add_bucket(i, _):
        slot = lax.rem(pair + i, bits)

        @pl.when((odd == 1) & (i == 0))
        def _():
            neighbour.wait_recv()

        for n in range(1, MIDDLE + 1):

            @pl.when((middle == n) & (i == odd))
            def _():
                part = recv3.at[pl.ds(0, n), pl.ds(0, GROUP - 1)]
                pltpu.make_async_remote_copy(
                    src_ref=part, dst_ref=part, send_sem=p3_send, recv_sem=p3_recv,
                    device_id={"ctx": lax.rem(me + 1, SHARDS)},
                ).wait_recv()

        @pl.when((pair == 1) & (i == bits - 1))
        def _():
            wait_bytes(recv1, GROUP, p4_sem.at[0], p4_sem.at[1]).wait_recv()

        for c in range(PIECES):
            q = jnp.concatenate([qt[c, 0], qt[c, 1]], axis=1)
            for g in range(4):
                bucket = recv3[slot, g * 4 : (g + 1) * 4].reshape(HALF, STATE)
                readout = jnp.dot(bucket, q, preferred_element_type=F32)
                for half in range(2):
                    lanes = slice(half * HALF, (half + 1) * HALF)
                    for h in range(2):
                        at = slice(h * HEAD_DIM, (h + 1) * HEAD_DIM)
                        to = slice(g * HALF + h * HEAD_DIM, g * HALF + (h + 1) * HEAD_DIM)
                        weight = slot_weight[2 * c + half, slot, 2 * g + h : 2 * g + h + 1]
                        mixed[c, half, to] = mixed[c, half, to] + readout[at, lanes] * weight
        return 0

    lax.fori_loop(0, bits, add_bucket, 0)

    def tokens_out(b):
        return pltpu.make_async_copy(out_ref.at[b], out_hbm.at[b], out_sem.at[b])

    for b in range(TOKENS // HALF):
        c, half = b // 2, b % 2
        square = jnp.zeros((HEAD_DIM, HALF), F32)
        for h in range(HEADS):
            part = mixed[c, half, h * HEAD_DIM : (h + 1) * HEAD_DIM]
            square = square + part * part
        mean = jnp.sum(square, axis=0, keepdims=True) * (1.0 / WIDTH)
        scale = lax.rsqrt(mean + 1e-05)
        out_ref[b] = (mixed[c, half] * scale * gain_col[...]).astype(BF16)
        tokens_out(b).start()

    @pl.when(me < SHARDS - 1)
    def _():
        to_next.wait_send()

    @pl.when(odd == 0)
    def _():
        neighbour.wait_send()

    @pl.when(pair == 0)
    def _():
        wait_bytes(recv1, GROUP, p4_sem.at[0], p4_sem.at[1]).wait_send()

    for n in range(MIDDLE + 1):

        @pl.when(middle == n)
        def _():
            for part in (stage.at[0], stage.at[1, pl.ds(0, GROUP // 2 - n)]):
                pltpu.make_async_remote_copy(
                    src_ref=part, dst_ref=part, send_sem=p3_send, recv_sem=p3_recv,
                    device_id={"ctx": lax.rem(me + 1, SHARDS)},
                ).wait_send()

    for b in range(TOKENS // HALF):
        tokens_out(b).wait()


def per_device(mixer_input, conv_weight, log_decay, level_weight, norm_gain):
    hbm = pl.BlockSpec(memory_space=pltpu.HBM)
    blocks = pl.pallas_call(
        kernel,
        out_shape=jax.ShapeDtypeStruct((TOKENS // HALF, WIDTH, HALF), BF16),
        in_specs=[hbm] * 5,
        out_specs=hbm,
        scratch_shapes=[
            pltpu.VMEM((TOKENS // HALF, WIDTH, HALF), BF16),
            pltpu.VMEM((TOKENS, WIDTH + 2 * STATE), BF16),
            pltpu.VMEM((4, WIDTH + 2 * STATE), F32),
            pltpu.VMEM((HEADS, TOKENS), F32),
            pltpu.VMEM((2 + BITS, HEADS, TOKENS), F32),
            pltpu.VMEM((1, WIDTH), F32),
            pltpu.VMEM((16, WIDTH + 2 * STATE), BF16),
            pltpu.VMEM((PIECES, 2, WIDTH, HALF), BF16),
            pltpu.VMEM((PIECES, STRETCH, STATE), BF16),
            pltpu.VMEM((PIECES, 2, STATE, HALF), BF16),
            pltpu.VMEM((PIECES, HEADS, STRETCH), F32),
            pltpu.VMEM((PIECES, STRETCH, HEADS), F32),
            pltpu.VMEM((PIECES, WIDTH, STATE), F32),
            pltpu.VMEM((PIECES - 1, WIDTH, STATE), BF16),
            pltpu.VMEM((PIECES, 2, WIDTH, HALF), F32),
            pltpu.VMEM((WIDTH, 1), F32),
            pltpu.VMEM((TOKENS // HALF, BITS, HEADS, HALF), F32),
            pltpu.VMEM((GROUP, ROWS, STATE), BF16),
            pltpu.VMEM((GROUP, ROWS, STATE), BF16),
            pltpu.VMEM((SHARDS, HEADS, HALF), F32),
            pltpu.VMEM((MIDDLE, GROUP, ROWS, STATE), BF16),
            pltpu.VMEM((ROWS, STATE), BF16),
            pltpu.VMEM((BITS, GROUP, ROWS, STATE), BF16),
            pltpu.SemaphoreType.DMA((4,)),
            pltpu.SemaphoreType.DMA((PIECES + 1,)),
            pltpu.SemaphoreType.DMA((TOKENS // HALF,)),
            pltpu.SemaphoreType.DMA((2,)),
            pltpu.SemaphoreType.DMA,
            pltpu.SemaphoreType.DMA,
            pltpu.SemaphoreType.DMA((4,)),
            pltpu.SemaphoreType.DMA((2,)),
            pltpu.SemaphoreType.DMA((2,)),
            pltpu.SemaphoreType.DMA,
            pltpu.SemaphoreType.DMA,
        ],
        compiler_params=pltpu.CompilerParams(
            collective_id=0, has_side_effects=True, vmem_limit_bytes=63 << 20
        ),
    )(mixer_input, conv_weight, log_decay, level_weight, norm_gain.reshape(1, WIDTH))
    return blocks.transpose(0, 2, 1).reshape(TOKENS, WIDTH)


def solution(mesh):
    placed = (
        P("ctx", "heads"),
        P(None, "heads"),
        P("heads", "ctx"),
        P(None, "heads", "ctx"),
        P("heads"),
    )
    return jax.shard_map(
        per_device, mesh=mesh, in_specs=placed, out_specs=P("ctx", "heads"), check_vma=False
    )
```

```python
import functools

import jax
import jax.numpy as jnp
from jax import lax
from jax.experimental import pallas as pl
from jax.experimental.pallas import tpu as pltpu
from jax.sharding import PartitionSpec as P

HEADS = 8
HEAD_DIM = 64
STATE = 128
STRETCH = 256
WIDTH = 512
TOKENS = 1024
PIECES = TOKENS // STRETCH
SHARDS = 32
ALONG_Z = 8
ALONG_Y = 4
OFFSETS = (4, 3, 5, 2, 6, 1, 7, 0)
ANSWERS = (5, 3, 6, 2, 7, 4, 1, 0)
BITS = 5
HALF = 128
GROUP = 16
ROWS = WIDTH // GROUP
MIDDLE = 3
LOG2E = 1.4426950408889634

NT = (((1,), (1,)), ((), ()))
F32 = jnp.float32
BF16 = jnp.bfloat16


def popcount(r):
    count = r % 2
    for k in range(1, BITS):
        count = count + (r // 2**k) % 2
    return count


def activate(window, conv_ref, cols):
    total = conv_ref[3:4, cols] * window[16:144]
    for j in range(3):
        total = total + conv_ref[j : j + 1, cols] * window[13 + j : 141 + j]
    half = 0.5 * total
    return (half + half * jnp.tanh(half)).astype(BF16)


def kernel(
    x_hbm, conv_hbm, rate_hbm, level_hbm, gain_hbm, out_hbm,
    out_ref, x_ref, conv_ref, rate_ref, level_ref, gain_ref, halo, xt, keys, qt, inner, column, state, low, mixed, gain_col, slot_weight,
    send1, recv1, spans, stage, top, recv3,
    in_sem, x_sem, out_sem, halo_sem, p1_send, p1_recv, span_sem, p0_sem, p4_sem, p3_send, p3_recv,
):
    me = lax.axis_index("ctx")
    bits = popcount(me)
    pair = me // GROUP
    place_in = lax.rem(me, GROUP)
    odd = lax.rem(me, 2)
    place_z = lax.rem(me, ALONG_Z)
    row_in = place_in // ALONG_Z
    middle = popcount(place_in // 2)

    barrier = pltpu.get_barrier_semaphore()

    small_in = [
        pltpu.make_async_copy(src, dst, in_sem.at[i])
        for i, (src, dst) in enumerate(
            ((rate_hbm, rate_ref), (conv_hbm, conv_ref), (gain_hbm, gain_ref), (level_hbm, level_ref))
        )
    ]

    def rows_in(start, count, at):
        span_of = pl.ds(start, count)
        return pltpu.make_async_copy(x_hbm.at[span_of], x_ref.at[span_of], x_sem.at[at])

    def stretch_in(c):
        return rows_in(pl.multiple_of(c * STRETCH - 16, 16), STRETCH, c)

    head_in = rows_in(0, STRETCH - 16, 0)
    tail_in = rows_in(TOKENS - 16, 16, PIECES)
    small_in[0].start()
    tail_in.start()
    stretch_in(PIECES - 1).start()

    def greet(d, _):
        other = lax.rem(me + d, SHARDS)
        pl.semaphore_signal(barrier, inc=1, device_id={"ctx": other})
        return 0

    lax.fori_loop(1, SHARDS, greet, 0)

    small_in[1].start()
    small_in[2].start()
    for c in range(PIECES - 2, 0, -1):
        stretch_in(c).start()
    head_in.start()
    small_in[3].start()

    small_in[0].wait()
    rows = lax.broadcasted_iota(jnp.int32, (STRETCH, STRETCH), 0)
    cols = lax.broadcasted_iota(jnp.int32, (STRETCH, STRETCH), 1)
    lower = jnp.where(rows >= cols, 1.0, 0.0).astype(F32)
    rates = jnp.concatenate(
        [rate_ref[:, c * STRETCH : (c + 1) * STRETCH] for c in range(PIECES)], axis=0
    )
    sums = lax.dot_general(
        rates * LOG2E, lower, NT, precision=lax.Precision.HIGHEST, preferred_element_type=F32
    )
    span = jnp.zeros((HEADS, HALF), F32)
    for c in range(PIECES):
        part = sums[c * HEADS : (c + 1) * HEADS]
        inner[c] = part
        span = span + jnp.broadcast_to(part[:, STRETCH - 1 :], (HEADS, HALF))
    spans[me] = span
    small_in[1].wait()

    row_start = me - lax.rem(me, ALONG_Z)

    def to_row(d):
        return row_start + lax.rem(me + d, ALONG_Z)

    def to_column(d):
        return lax.rem(me + d * ALONG_Z, SHARDS)

    def span_along_row(d):
        return pltpu.make_async_remote_copy(
            src_ref=spans.at[me], dst_ref=spans.at[me],
            send_sem=span_sem.at[0], recv_sem=span_sem.at[1], device_id={"ctx": to_row(d)},
        )

    def span_along_column(d):
        at = pl.ds(row_start, ALONG_Z)
        return pltpu.make_async_remote_copy(
            src_ref=spans.at[at], dst_ref=spans.at[at],
            send_sem=span_sem.at[2], recv_sem=span_sem.at[3], device_id={"ctx": to_column(d)},
        )

    def wait_bytes(ref, count, send_sem, recv_sem):
        part = ref.at[pl.ds(0, count)]
        return pltpu.make_async_remote_copy(
            src_ref=part, dst_ref=part, send_sem=send_sem, recv_sem=recv_sem,
            device_id={"ctx": lax.rem(me + 1, SHARDS)},
        )

    to_next = pltpu.make_async_remote_copy(
        src_ref=x_ref.at[pl.ds(TOKENS - 16, 16)], dst_ref=halo,
        send_sem=halo_sem.at[0], recv_sem=halo_sem.at[1],
        device_id={"ctx": lax.rem(me + 1, SHARDS)},
    )

    def place(b, group, act):
        c, half = b // 2, b % 2
        if group < 4:
            xt[c, half, group * HALF : (group + 1) * HALF] = act.T
        elif group == 4:
            keys[c, pl.ds(pl.multiple_of(half * HALF, HALF), HALF)] = act
        else:
            qt[c, half] = act.T

    def block(b):
        start = pl.multiple_of(b * HALF - 16, 16)
        for group in range(6):
            chans = slice(group * HALF, (group + 1) * HALF)
            window = x_ref[pl.ds(start, HALF + 16), chans].astype(F32)
            place(b, group, activate(window, conv_ref, chans))

    def stretch_state(c):
        to_end = jnp.exp2(inner[c, :, STRETCH - 1 :] - inner[c])
        parts = []
        for h in range(HEADS):
            x_h = jnp.concatenate(
                [xt[c, 0, h * HEAD_DIM : (h + 1) * HEAD_DIM], xt[c, 1, h * HEAD_DIM : (h + 1) * HEAD_DIM]],
                axis=1,
            )
            parts.append((x_h.astype(F32) * to_end[h : h + 1]).astype(BF16))
        state[c] = jnp.dot(
            jnp.concatenate(parts, axis=0), keys[c], preferred_element_type=F32
        )

    tail_in.wait()

    def late(i, _):
        c = PIECES - 1 - i
        stretch_in(c).wait()
        lax.fori_loop(0, 2, lambda half, _: (block(2 * c + 1 - half), 0)[1], 0)
        stretch_state(c)

        @pl.when(i == 0)
        def _():
            pl.semaphore_wait(barrier, SHARDS - 1)

            @pl.when(me < SHARDS - 1)
            def _():
                to_next.start()

            for d in range(1, ALONG_Z):
                span_along_row(d).start()

        return 0

    lax.fori_loop(0, PIECES - 1, late, 0)
    head_in.wait()
    block(1)

    @pl.when(me == 0)
    def _():
        halo[...] = jnp.zeros_like(halo)

    @pl.when(me > 0)
    def _():
        to_next.wait_recv()


    for group in range(6):
        chans = slice(group * HALF, (group + 1) * HALF)
        window = jnp.concatenate([halo[:, chans], x_ref[:HALF, chans]], axis=0).astype(F32)
        place(0, group, activate(window, conv_ref, chans))
    stretch_state(0)

    for h in range(HEADS):
        at = slice(h * HEAD_DIM, (h + 1) * HEAD_DIM)
        carried = state[0, at]
        for c in range(1, PIECES):
            low[c - 1, at] = carried.astype(BF16)
            fall = jnp.exp2(
                jnp.broadcast_to(inner[c, h : h + 1, STRETCH - 1 :], (1, STATE))
            )
            carried = fall * carried + state[c, at]
        send1[2 * h : 2 * (h + 1)] = carried.astype(BF16).reshape(2, ROWS, STATE)

    def across(along, down):
        return (row_in + down) % 2 * ALONG_Z + lax.rem(place_z + along, ALONG_Z)

    for along in OFFSETS:
        for down in (0, 1):
            if along or down:
                there = across(along, down)
                pltpu.make_async_remote_copy(
                    src_ref=send1.at[there], dst_ref=recv1.at[place_in],
                    send_sem=p1_send, recv_sem=p1_recv, device_id={"ctx": pair * GROUP + there},
                ).start()

    recv1[place_in] = send1[place_in]

    small_in[2].wait()
    diag = (rows == cols)[:HALF, :HALF]
    for g in range(WIDTH // HALF):
        row = jnp.broadcast_to(gain_ref[:, g * HALF : (g + 1) * HALF], (HALF, HALF))
        gain_col[g * HALF : (g + 1) * HALF] = jnp.sum(
            jnp.where(diag, row, 0.0), axis=1, keepdims=True
        )
    for c in range(PIECES):
        column[c] = inner[c].T
    causal = (rows <= cols)[:HALF, :HALF]

    def near_own(c, before):
        q = [qt[c, 0], qt[c, 1]]
        k = keys[c]
        for half in range(2):
            width = HALF * (half + 1)
            score = jnp.dot(k[:width], q[half], preferred_element_type=F32)
            at_t = pl.ds(pl.multiple_of(c * STRETCH, STRETCH) + half * HALF, HALF)
            row_all = inner[c, :, half * HALF : (half + 1) * HALF]
            own_scale = level_ref[0, :, at_t]
            near_scale = level_ref[1, :, at_t] * jnp.exp2(row_all)
            if before:
                readout = jnp.dot(low[c - 1], q[half], preferred_element_type=F32)
            for h in range(HEADS):
                at = slice(h * HEAD_DIM, (h + 1) * HEAD_DIM)
                gap = row_all[h : h + 1] - column[c, :width, h : h + 1]
                blocks = []
                if half == 1:
                    blocks.append((jnp.exp2(gap[:HALF]) * score[:HALF]).astype(BF16))
                last = jnp.where(causal, gap[width - HALF :], -jnp.inf)
                blocks.append((jnp.exp2(last) * score[width - HALF :]).astype(BF16))
                own = jnp.dot(xt[c, half, at], blocks[-1], preferred_element_type=F32)
                if half == 1:
                    own = own + jnp.dot(xt[c, 0, at], blocks[0], preferred_element_type=F32)
                own = own * own_scale[h : h + 1]
                if before:
                    own = own + readout[at] * near_scale[h : h + 1]
                mixed[c, half, at] = own

    neighbour = pltpu.make_async_remote_copy(
        src_ref=send1, dst_ref=recv3.at[pair],
        send_sem=p0_sem.at[0], recv_sem=p0_sem.at[1],
        device_id={"ctx": lax.rem(me + 1, SHARDS)},
    )

    @pl.when(odd == 0)
    def _():
        neighbour.start()

    small_in[3].wait()
    near_own(0, False)
    wait_bytes(spans, ALONG_Z - 1, span_sem.at[0], span_sem.at[1]).wait()
    for d in range(1, ALONG_Y):
        span_along_column(d).start()

    def rest(c, _):
        near_own(c, True)

        return 0

    lax.fori_loop(1, PIECES, rest, 0)

    wait_bytes(recv1, GROUP - 1, p1_send, p1_recv).wait()
    wait_bytes(spans, SHARDS - ALONG_Z, span_sem.at[2], span_sem.at[3]).wait()
    head = place_in // (GROUP // HEADS)
    ends = [recv1[q].astype(F32) for q in range(GROUP)]
    falls = [spans[pair * GROUP + q, pl.ds(head, 1)] for q in range(GROUP)]
    for k in range(BITS - 1):
        if k > 0:
            for group in range(0, len(ends), 2):
                left = ends[group].astype(BF16)
                for r in range((group + 1) << k, (group + 2) << k):
                    stage[popcount((r // 2) % 2 ** (k - 1)), r] = left
        ends = [
            jnp.exp2(falls[i + 1]) * ends[i] + ends[i + 1] for i in range(0, len(ends), 2)
        ]
        falls = [falls[i] + falls[i + 1] for i in range(0, len(falls), 2)]
    top[...] = ends[0].astype(BF16)

    def answer(there):
        @pl.when(pair == 0)
        def _():
            pltpu.make_async_remote_copy(
                src_ref=top, dst_ref=recv3.at[0, place_in],
                send_sem=p4_sem.at[0], recv_sem=p4_sem.at[1],
                device_id={"ctx": GROUP + there},
            ).start()

        count = popcount(there // 2) * jnp.where(there == place_in, 0, 1)
        for n in range(1, MIDDLE + 1):

            @pl.when(count == n)
            def _():
                pltpu.make_async_remote_copy(
                    src_ref=stage.at[pl.ds(0, n), there],
                    dst_ref=recv3.at[pl.ds(pair + lax.rem(there, 2), n), place_in],
                    send_sem=p3_send, recv_sem=p3_recv,
                    device_id={"ctx": pair * GROUP + there},
                ).start()


    for t in range(4):
        turn = lax.rem(place_in + t, 4)
        answer(turn // 2 * ALONG_Z + turn % 2)
    for along in ANSWERS:
        for down in (1, 0):
            there = across(along, down)

            @pl.when(lax.rem(there, ALONG_Z) >= 2)
            def _(there=there):
                answer(there)

    for n in range(1, MIDDLE + 1):

        @pl.when(middle == n)
        def _():
            recv3[pl.ds(pair + odd, n), place_in] = stage[:n, place_in]

    for k in range(BITS):
        digit = (me // 2**k) % 2
        if k == 0:
            slot = pair
        elif k == BITS - 1:
            slot = 0
        else:
            slot = pair + odd + popcount((me // 2) % 2 ** (k - 1))
        first = (me // 2**k) * 2**k

        @pl.when(digit == 1)
        def _():
            def add(q, total):
                return total + spans[q]

            between = lax.fori_loop(first, me, add, jnp.zeros((HEADS, HALF), F32))
            for c in range(PIECES):
                gap = between + jnp.zeros((HEADS, HALF), F32)
                for e in range(c):
                    gap = gap + jnp.broadcast_to(inner[e, :, STRETCH - 1 :], (HEADS, HALF))
                for half in range(2):
                    tokens = slice((2 * c + half) * HALF, (2 * c + half + 1) * HALF)
                    slot_weight[2 * c + half, slot] = level_ref[2 + k, :, tokens] * jnp.exp2(
                        gap + inner[c, :, half * HALF : (half + 1) * HALF]
                    )

    def add_bucket(i, _):
        slot = lax.rem(pair + i, bits)

        @pl.when((odd == 1) & (i == 0))
        def _():
            neighbour.wait_recv()

        for n in range(1, MIDDLE + 1):

            @pl.when((middle == n) & (i == odd))
            def _():
                part = recv3.at[pl.ds(0, n), pl.ds(0, GROUP - 1)]
                pltpu.make_async_remote_copy(
                    src_ref=part, dst_ref=part, send_sem=p3_send, recv_sem=p3_recv,
                    device_id={"ctx": lax.rem(me + 1, SHARDS)},
                ).wait_recv()

        @pl.when((pair == 1) & (i == bits - 1))
        def _():
            wait_bytes(recv1, GROUP, p4_sem.at[0], p4_sem.at[1]).wait_recv()

        for c in range(PIECES):
            q = jnp.concatenate([qt[c, 0], qt[c, 1]], axis=1)
            for g in range(4):
                bucket = recv3[slot, g * 4 : (g + 1) * 4].reshape(HALF, STATE)
                readout = jnp.dot(bucket, q, preferred_element_type=F32)
                for half in range(2):
                    lanes = slice(half * HALF, (half + 1) * HALF)
                    for h in range(2):
                        at = slice(h * HEAD_DIM, (h + 1) * HEAD_DIM)
                        to = slice(g * HALF + h * HEAD_DIM, g * HALF + (h + 1) * HEAD_DIM)
                        weight = slot_weight[2 * c + half, slot, 2 * g + h : 2 * g + h + 1]
                        mixed[c, half, to] = mixed[c, half, to] + readout[at, lanes] * weight
        return 0

    lax.fori_loop(0, bits, add_bucket, 0)

    def tokens_out(b):
        return pltpu.make_async_copy(out_ref.at[b], out_hbm.at[b], out_sem.at[b])

    for b in range(TOKENS // HALF):
        c, half = b // 2, b % 2
        square = jnp.zeros((HEAD_DIM, HALF), F32)
        for h in range(HEADS):
            part = mixed[c, half, h * HEAD_DIM : (h + 1) * HEAD_DIM]
            square = square + part * part
        mean = jnp.sum(square, axis=0, keepdims=True) * (1.0 / WIDTH)
        scale = lax.rsqrt(mean + 1e-05)
        out_ref[b] = (mixed[c, half] * scale * gain_col[...]).astype(BF16)
        tokens_out(b).start()

    @pl.when(me < SHARDS - 1)
    def _():
        to_next.wait_send()

    @pl.when(odd == 0)
    def _():
        neighbour.wait_send()

    @pl.when(pair == 0)
    def _():
        wait_bytes(recv1, GROUP, p4_sem.at[0], p4_sem.at[1]).wait_send()

    for n in range(MIDDLE + 1):

        @pl.when(middle == n)
        def _():
            for part in (stage.at[0], stage.at[1, pl.ds(0, GROUP // 2 - n)]):
                pltpu.make_async_remote_copy(
                    src_ref=part, dst_ref=part, send_sem=p3_send, recv_sem=p3_recv,
                    device_id={"ctx": lax.rem(me + 1, SHARDS)},
                ).wait_send()

    for b in range(TOKENS // HALF):
        tokens_out(b).wait()


def per_device(mixer_input, conv_weight, log_decay, level_weight, norm_gain):
    hbm = pl.BlockSpec(memory_space=pltpu.HBM)
    blocks = pl.pallas_call(
        kernel,
        out_shape=jax.ShapeDtypeStruct((TOKENS // HALF, WIDTH, HALF), BF16),
        in_specs=[hbm] * 5,
        out_specs=hbm,
        scratch_shapes=[
            pltpu.VMEM((TOKENS // HALF, WIDTH, HALF), BF16),
            pltpu.VMEM((TOKENS, WIDTH + 2 * STATE), BF16),
            pltpu.VMEM((4, WIDTH + 2 * STATE), F32),
            pltpu.VMEM((HEADS, TOKENS), F32),
            pltpu.VMEM((2 + BITS, HEADS, TOKENS), F32),
            pltpu.VMEM((1, WIDTH), F32),
            pltpu.VMEM((16, WIDTH + 2 * STATE), BF16),
            pltpu.VMEM((PIECES, 2, WIDTH, HALF), BF16),
            pltpu.VMEM((PIECES, STRETCH, STATE), BF16),
            pltpu.VMEM((PIECES, 2, STATE, HALF), BF16),
            pltpu.VMEM((PIECES, HEADS, STRETCH), F32),
            pltpu.VMEM((PIECES, STRETCH, HEADS), F32),
            pltpu.VMEM((PIECES, WIDTH, STATE), F32),
            pltpu.VMEM((PIECES - 1, WIDTH, STATE), BF16),
            pltpu.VMEM((PIECES, 2, WIDTH, HALF), F32),
            pltpu.VMEM((WIDTH, 1), F32),
            pltpu.VMEM((TOKENS // HALF, BITS, HEADS, HALF), F32),
            pltpu.VMEM((GROUP, ROWS, STATE), BF16),
            pltpu.VMEM((GROUP, ROWS, STATE), BF16),
            pltpu.VMEM((SHARDS, HEADS, HALF), F32),
            pltpu.VMEM((MIDDLE, GROUP, ROWS, STATE), BF16),
            pltpu.VMEM((ROWS, STATE), BF16),
            pltpu.VMEM((BITS, GROUP, ROWS, STATE), BF16),
            pltpu.SemaphoreType.DMA((4,)),
            pltpu.SemaphoreType.DMA((PIECES + 1,)),
            pltpu.SemaphoreType.DMA((TOKENS // HALF,)),
            pltpu.SemaphoreType.DMA((2,)),
            pltpu.SemaphoreType.DMA,
            pltpu.SemaphoreType.DMA,
            pltpu.SemaphoreType.DMA((4,)),
            pltpu.SemaphoreType.DMA((2,)),
            pltpu.SemaphoreType.DMA((2,)),
            pltpu.SemaphoreType.DMA,
            pltpu.SemaphoreType.DMA,
        ],
        compiler_params=pltpu.CompilerParams(
            collective_id=0, has_side_effects=True, vmem_limit_bytes=63 << 20
        ),
    )(mixer_input, conv_weight, log_decay, level_weight, norm_gain.reshape(1, WIDTH))
    return blocks.transpose(0, 2, 1).reshape(TOKENS, WIDTH)


def solution(mesh):
    placed = (
        P("ctx", "heads"),
        P(None, "heads"),
        P("heads", "ctx"),
        P(None, "heads", "ctx"),
        P("heads"),
    )
    return jax.shard_map(
        per_device, mesh=mesh, in_specs=placed, out_specs=P("ctx", "heads"), check_vma=False
    )
```

```python
import functools

import jax
import jax.numpy as jnp
from jax import lax
from jax.experimental import pallas as pl
from jax.experimental.pallas import tpu as pltpu
from jax.sharding import PartitionSpec as P

HEADS = 8
HEAD_DIM = 64
STATE = 128
STRETCH = 256
WIDTH = 512
TOKENS = 1024
PIECES = TOKENS // STRETCH
SHARDS = 32
ALONG_Z = 8
ALONG_Y = 4
OFFSETS = (4, 3, 5, 2, 6, 1, 7, 0)
ANSWERS = (5, 3, 6, 2, 7, 4, 1, 0)
BITS = 5
HALF = 128
GROUP = 16
ROWS = WIDTH // GROUP
MIDDLE = 3
LOG2E = 1.4426950408889634

NT = (((1,), (1,)), ((), ()))
F32 = jnp.float32
BF16 = jnp.bfloat16


def popcount(r):
    count = r % 2
    for k in range(1, BITS):
        count = count + (r // 2**k) % 2
    return count


def activate(window, conv_ref, cols):
    total = conv_ref[3:4, cols] * window[16:144]
    for j in range(3):
        total = total + conv_ref[j : j + 1, cols] * window[13 + j : 141 + j]
    half = 0.5 * total
    return (half + half * jnp.tanh(half)).astype(BF16)


def kernel(
    x_hbm, conv_hbm, rate_hbm, level_hbm, gain_hbm, out_hbm,
    out_ref, x_ref, conv_ref, rate_ref, level_ref, gain_ref, halo, xt, keys, qt, inner, column, state, low, mixed, gain_col, slot_weight,
    send1, recv1, spans, stage, top, recv3,
    in_sem, x_sem, out_sem, halo_sem, p1_send, p1_recv, span_sem, p0_sem, p4_sem, p3_send, p3_recv,
):
    me = lax.axis_index("ctx")
    bits = popcount(me)
    pair = me // GROUP
    place_in = lax.rem(me, GROUP)
    odd = lax.rem(me, 2)
    place_z = lax.rem(me, ALONG_Z)
    row_in = place_in // ALONG_Z
    middle = popcount(place_in // 2)

    barrier = pltpu.get_barrier_semaphore()

    small_in = [
        pltpu.make_async_copy(src, dst, in_sem.at[i])
        for i, (src, dst) in enumerate(
            ((rate_hbm, rate_ref), (conv_hbm, conv_ref), (gain_hbm, gain_ref), (level_hbm, level_ref))
        )
    ]

    def rows_in(start, count, at):
        span_of = pl.ds(start, count)
        return pltpu.make_async_copy(x_hbm.at[span_of], x_ref.at[span_of], x_sem.at[at])

    def stretch_in(c):
        return rows_in(pl.multiple_of(c * STRETCH - 16, 16), STRETCH, c)

    head_in = rows_in(0, STRETCH - 16, 0)
    tail_in = rows_in(TOKENS - 16, 16, PIECES)
    small_in[0].start()
    tail_in.start()
    stretch_in(PIECES - 1).start()

    def greet(d, _):
        other = lax.rem(me + d, SHARDS)
        pl.semaphore_signal(barrier, inc=1, device_id={"ctx": other})
        return 0

    lax.fori_loop(1, SHARDS, greet, 0)

    small_in[1].start()
    small_in[2].start()
    for c in range(PIECES - 2, 0, -1):
        stretch_in(c).start()
    head_in.start()
    small_in[3].start()

    small_in[0].wait()
    rows = lax.broadcasted_iota(jnp.int32, (STRETCH, STRETCH), 0)
    cols = lax.broadcasted_iota(jnp.int32, (STRETCH, STRETCH), 1)
    lower = jnp.where(rows >= cols, 1.0, 0.0).astype(F32)
    rates = jnp.concatenate(
        [rate_ref[:, c * STRETCH : (c + 1) * STRETCH] for c in range(PIECES)], axis=0
    )
    sums = lax.dot_general(
        rates * LOG2E, lower, NT, precision=lax.Precision.HIGHEST, preferred_element_type=F32
    )
    span = jnp.zeros((HEADS, HALF), F32)
    for c in range(PIECES):
        part = sums[c * HEADS : (c + 1) * HEADS]
        inner[c] = part
        span = span + jnp.broadcast_to(part[:, STRETCH - 1 :], (HEADS, HALF))
    spans[me] = span
    small_in[1].wait()

    row_start = me - lax.rem(me, ALONG_Z)

    def to_row(d):
        return row_start + lax.rem(me + d, ALONG_Z)

    def to_column(d):
        return lax.rem(me + d * ALONG_Z, SHARDS)

    def span_along_row(d):
        return pltpu.make_async_remote_copy(
            src_ref=spans.at[me], dst_ref=spans.at[me],
            send_sem=span_sem.at[0], recv_sem=span_sem.at[1], device_id={"ctx": to_row(d)},
        )

    def span_along_column(d):
        at = pl.ds(row_start, ALONG_Z)
        return pltpu.make_async_remote_copy(
            src_ref=spans.at[at], dst_ref=spans.at[at],
            send_sem=span_sem.at[2], recv_sem=span_sem.at[3], device_id={"ctx": to_column(d)},
        )

    def wait_bytes(ref, count, send_sem, recv_sem):
        part = ref.at[pl.ds(0, count)]
        return pltpu.make_async_remote_copy(
            src_ref=part, dst_ref=part, send_sem=send_sem, recv_sem=recv_sem,
            device_id={"ctx": lax.rem(me + 1, SHARDS)},
        )

    to_next = pltpu.make_async_remote_copy(
        src_ref=x_ref.at[pl.ds(TOKENS - 16, 16)], dst_ref=halo,
        send_sem=halo_sem.at[0], recv_sem=halo_sem.at[1],
        device_id={"ctx": lax.rem(me + 1, SHARDS)},
    )

    def place(b, group, act):
        c, half = b // 2, b % 2
        if group < 4:
            xt[c, half, group * HALF : (group + 1) * HALF] = act.T
        elif group == 4:
            keys[c, pl.ds(pl.multiple_of(half * HALF, HALF), HALF)] = act
        else:
            qt[c, half] = act.T

    def block(b):
        start = pl.multiple_of(b * HALF - 16, 16)
        for group in range(6):
            chans = slice(group * HALF, (group + 1) * HALF)
            window = x_ref[pl.ds(start, HALF + 16), chans].astype(F32)
            place(b, group, activate(window, conv_ref, chans))

    def stretch_state(c):
        to_end = jnp.exp2(inner[c, :, STRETCH - 1 :] - inner[c])
        parts = []
        for h in range(HEADS):
            x_h = jnp.concatenate(
                [xt[c, 0, h * HEAD_DIM : (h + 1) * HEAD_DIM], xt[c, 1, h * HEAD_DIM : (h + 1) * HEAD_DIM]],
                axis=1,
            )
            parts.append((x_h.astype(F32) * to_end[h : h + 1]).astype(BF16))
        state[c] = jnp.dot(
            jnp.concatenate(parts, axis=0), keys[c], preferred_element_type=F32
        )

    tail_in.wait()

    def late(i, _):
        c = PIECES - 1 - i
        stretch_in(c).wait()
        lax.fori_loop(0, 2, lambda half, _: (block(2 * c + 1 - half), 0)[1], 0)
        stretch_state(c)

        @pl.when(i == 0)
        def _():
            pl.semaphore_wait(barrier, SHARDS - 1)

            @pl.when(me < SHARDS - 1)
            def _():
                to_next.start()

            for d in range(1, ALONG_Z):
                span_along_row(d).start()

        return 0

    lax.fori_loop(0, PIECES - 1, late, 0)
    head_in.wait()
    block(1)

    @pl.when(me == 0)
    def _():
        halo[...] = jnp.zeros_like(halo)

    @pl.when(me > 0)
    def _():
        to_next.wait_recv()


    for group in range(6):
        chans = slice(group * HALF, (group + 1) * HALF)
        window = jnp.concatenate([halo[:, chans], x_ref[:HALF, chans]], axis=0).astype(F32)
        place(0, group, activate(window, conv_ref, chans))
    stretch_state(0)

    for h in range(HEADS):
        at = slice(h * HEAD_DIM, (h + 1) * HEAD_DIM)
        carried = state[0, at]
        for c in range(1, PIECES):
            low[c - 1, at] = carried.astype(BF16)
            fall = jnp.exp2(
                jnp.broadcast_to(inner[c, h : h + 1, STRETCH - 1 :], (1, STATE))
            )
            carried = fall * carried + state[c, at]
        send1[2 * h : 2 * (h + 1)] = carried.astype(BF16).reshape(2, ROWS, STATE)

    def across(along, down):
        return (row_in + down) % 2 * ALONG_Z + lax.rem(place_z + along, ALONG_Z)

    for along in OFFSETS:
        for down in (0, 1):
            if along or down:
                there = across(along, down)
                pltpu.make_async_remote_copy(
                    src_ref=send1.at[there], dst_ref=recv1.at[place_in],
                    send_sem=p1_send, recv_sem=p1_recv, device_id={"ctx": pair * GROUP + there},
                ).start()

    recv1[place_in] = send1[place_in]

    small_in[2].wait()
    diag = (rows == cols)[:HALF, :HALF]
    for g in range(WIDTH // HALF):
        row = jnp.broadcast_to(gain_ref[:, g * HALF : (g + 1) * HALF], (HALF, HALF))
        gain_col[g * HALF : (g + 1) * HALF] = jnp.sum(
            jnp.where(diag, row, 0.0), axis=1, keepdims=True
        )
    for c in range(PIECES):
        column[c] = inner[c].T
    causal = (rows <= cols)[:HALF, :HALF]

    def near_own(c, before):
        q = [qt[c, 0], qt[c, 1]]
        k = keys[c]
        for half in range(2):
            width = HALF * (half + 1)
            score = jnp.dot(k[:width], q[half], preferred_element_type=F32)
            at_t = pl.ds(pl.multiple_of(c * STRETCH, STRETCH) + half * HALF, HALF)
            row_all = inner[c, :, half * HALF : (half + 1) * HALF]
            own_scale = level_ref[0, :, at_t]
            near_scale = level_ref[1, :, at_t] * jnp.exp2(row_all)
            if before:
                readout = jnp.dot(low[c - 1], q[half], preferred_element_type=F32)
            for h in range(HEADS):
                at = slice(h * HEAD_DIM, (h + 1) * HEAD_DIM)
                gap = row_all[h : h + 1] - column[c, :width, h : h + 1]
                blocks = []
                if half == 1:
                    blocks.append((jnp.exp2(gap[:HALF]) * score[:HALF]).astype(BF16))
                last = jnp.where(causal, gap[width - HALF :], -jnp.inf)
                blocks.append((jnp.exp2(last) * score[width - HALF :]).astype(BF16))
                own = jnp.dot(xt[c, half, at], blocks[-1], preferred_element_type=F32)
                if half == 1:
                    own = own + jnp.dot(xt[c, 0, at], blocks[0], preferred_element_type=F32)
                own = own * own_scale[h : h + 1]
                if before:
                    own = own + readout[at] * near_scale[h : h + 1]
                mixed[c, half, at] = own

    neighbour = pltpu.make_async_remote_copy(
        src_ref=send1, dst_ref=recv3.at[pair],
        send_sem=p0_sem.at[0], recv_sem=p0_sem.at[1],
        device_id={"ctx": lax.rem(me + 1, SHARDS)},
    )

    @pl.when(odd == 0)
    def _():
        neighbour.start()

    small_in[3].wait()
    near_own(0, False)
    wait_bytes(spans, ALONG_Z - 1, span_sem.at[0], span_sem.at[1]).wait()
    for d in range(1, ALONG_Y):
        span_along_column(d).start()

    def rest(c, _):
        near_own(c, True)

        return 0

    lax.fori_loop(1, PIECES, rest, 0)

    wait_bytes(recv1, GROUP - 1, p1_send, p1_recv).wait()
    wait_bytes(spans, SHARDS - ALONG_Z, span_sem.at[2], span_sem.at[3]).wait()
    head = place_in // (GROUP // HEADS)
    ends = [recv1[q].astype(F32) for q in range(GROUP)]
    falls = [spans[pair * GROUP + q, pl.ds(head, 1)] for q in range(GROUP)]
    for k in range(BITS - 1):
        if k > 0:
            for group in range(0, len(ends), 2):
                left = ends[group].astype(BF16)
                for r in range((group + 1) << k, (group + 2) << k):
                    stage[popcount((r // 2) % 2 ** (k - 1)), r] = left
        ends = [
            jnp.exp2(falls[i + 1]) * ends[i] + ends[i + 1] for i in range(0, len(ends), 2)
        ]
        falls = [falls[i] + falls[i + 1] for i in range(0, len(falls), 2)]
    top[...] = ends[0].astype(BF16)

    def answer(there):
        @pl.when(pair == 0)
        def _():
            pltpu.make_async_remote_copy(
                src_ref=top, dst_ref=recv3.at[0, place_in],
                send_sem=p4_sem.at[0], recv_sem=p4_sem.at[1],
                device_id={"ctx": GROUP + there},
            ).start()

        count = popcount(there // 2) * jnp.where(there == place_in, 0, 1)
        for n in range(1, MIDDLE + 1):

            @pl.when(count == n)
            def _():
                pltpu.make_async_remote_copy(
                    src_ref=stage.at[pl.ds(0, n), there],
                    dst_ref=recv3.at[pl.ds(pair + lax.rem(there, 2), n), place_in],
                    send_sem=p3_send, recv_sem=p3_recv,
                    device_id={"ctx": pair * GROUP + there},
                ).start()


    for t in range(4):
        turn = lax.rem(place_in + t, 4)
        answer(turn // 2 * ALONG_Z + turn % 2)
    for k in range(BITS):
        digit = (me // 2**k) % 2
        if k == 0:
            slot = pair
        elif k == BITS - 1:
            slot = 0
        else:
            slot = pair + odd + popcount((me // 2) % 2 ** (k - 1))
        first = (me // 2**k) * 2**k

        @pl.when(digit == 1)
        def _():
            def add(q, total):
                return total + spans[q]

            between = lax.fori_loop(first, me, add, jnp.zeros((HEADS, HALF), F32))
            for c in range(PIECES):
                gap = between + jnp.zeros((HEADS, HALF), F32)
                for e in range(c):
                    gap = gap + jnp.broadcast_to(inner[e, :, STRETCH - 1 :], (HEADS, HALF))
                for half in range(2):
                    tokens = slice((2 * c + half) * HALF, (2 * c + half + 1) * HALF)
                    slot_weight[2 * c + half, slot] = level_ref[2 + k, :, tokens] * jnp.exp2(
                        gap + inner[c, :, half * HALF : (half + 1) * HALF]
                    )

    for along in ANSWERS:
        for down in (1, 0):
            there = across(along, down)

            @pl.when(lax.rem(there, ALONG_Z) >= 2)
            def _(there=there):
                answer(there)

    for n in range(1, MIDDLE + 1):

        @pl.when(middle == n)
        def _():
            recv3[pl.ds(pair + odd, n), place_in] = stage[:n, place_in]

    def add_bucket(i, _):
        slot = lax.rem(pair + i, bits)

        @pl.when((odd == 1) & (i == 0))
        def _():
            neighbour.wait_recv()

        for n in range(1, MIDDLE + 1):

            @pl.when((middle == n) & (i == odd))
            def _():
                part = recv3.at[pl.ds(0, n), pl.ds(0, GROUP - 1)]
                pltpu.make_async_remote_copy(
                    src_ref=part, dst_ref=part, send_sem=p3_send, recv_sem=p3_recv,
                    device_id={"ctx": lax.rem(me + 1, SHARDS)},
                ).wait_recv()

        @pl.when((pair == 1) & (i == bits - 1))
        def _():
            wait_bytes(recv1, GROUP, p4_sem.at[0], p4_sem.at[1]).wait_recv()

        for c in range(PIECES):
            q = jnp.concatenate([qt[c, 0], qt[c, 1]], axis=1)
            for g in range(4):
                bucket = recv3[slot, g * 4 : (g + 1) * 4].reshape(HALF, STATE)
                readout = jnp.dot(bucket, q, preferred_element_type=F32)
                for half in range(2):
                    lanes = slice(half * HALF, (half + 1) * HALF)
                    for h in range(2):
                        at = slice(h * HEAD_DIM, (h + 1) * HEAD_DIM)
                        to = slice(g * HALF + h * HEAD_DIM, g * HALF + (h + 1) * HEAD_DIM)
                        weight = slot_weight[2 * c + half, slot, 2 * g + h : 2 * g + h + 1]
                        mixed[c, half, to] = mixed[c, half, to] + readout[at, lanes] * weight
        return 0

    lax.fori_loop(0, bits, add_bucket, 0)

    def tokens_out(b):
        return pltpu.make_async_copy(out_ref.at[b], out_hbm.at[b], out_sem.at[b])

    for b in range(TOKENS // HALF):
        c, half = b // 2, b % 2
        square = jnp.zeros((HEAD_DIM, HALF), F32)
        for h in range(HEADS):
            part = mixed[c, half, h * HEAD_DIM : (h + 1) * HEAD_DIM]
            square = square + part * part
        mean = jnp.sum(square, axis=0, keepdims=True) * (1.0 / WIDTH)
        scale = lax.rsqrt(mean + 1e-05)
        out_ref[b] = (mixed[c, half] * scale * gain_col[...]).astype(BF16)
        tokens_out(b).start()

    @pl.when(me < SHARDS - 1)
    def _():
        to_next.wait_send()

    @pl.when(odd == 0)
    def _():
        neighbour.wait_send()

    @pl.when(pair == 0)
    def _():
        wait_bytes(recv1, GROUP, p4_sem.at[0], p4_sem.at[1]).wait_send()

    for n in range(MIDDLE + 1):

        @pl.when(middle == n)
        def _():
            for part in (stage.at[0], stage.at[1, pl.ds(0, GROUP // 2 - n)]):
                pltpu.make_async_remote_copy(
                    src_ref=part, dst_ref=part, send_sem=p3_send, recv_sem=p3_recv,
                    device_id={"ctx": lax.rem(me + 1, SHARDS)},
                ).wait_send()

    for b in range(TOKENS // HALF):
        tokens_out(b).wait()


def per_device(mixer_input, conv_weight, log_decay, level_weight, norm_gain):
    hbm = pl.BlockSpec(memory_space=pltpu.HBM)
    blocks = pl.pallas_call(
        kernel,
        out_shape=jax.ShapeDtypeStruct((TOKENS // HALF, WIDTH, HALF), BF16),
        in_specs=[hbm] * 5,
        out_specs=hbm,
        scratch_shapes=[
            pltpu.VMEM((TOKENS // HALF, WIDTH, HALF), BF16),
            pltpu.VMEM((TOKENS, WIDTH + 2 * STATE), BF16),
            pltpu.VMEM((4, WIDTH + 2 * STATE), F32),
            pltpu.VMEM((HEADS, TOKENS), F32),
            pltpu.VMEM((2 + BITS, HEADS, TOKENS), F32),
            pltpu.VMEM((1, WIDTH), F32),
            pltpu.VMEM((16, WIDTH + 2 * STATE), BF16),
            pltpu.VMEM((PIECES, 2, WIDTH, HALF), BF16),
            pltpu.VMEM((PIECES, STRETCH, STATE), BF16),
            pltpu.VMEM((PIECES, 2, STATE, HALF), BF16),
            pltpu.VMEM((PIECES, HEADS, STRETCH), F32),
            pltpu.VMEM((PIECES, STRETCH, HEADS), F32),
            pltpu.VMEM((PIECES, WIDTH, STATE), F32),
            pltpu.VMEM((PIECES - 1, WIDTH, STATE), BF16),
            pltpu.VMEM((PIECES, 2, WIDTH, HALF), F32),
            pltpu.VMEM((WIDTH, 1), F32),
            pltpu.VMEM((TOKENS // HALF, BITS, HEADS, HALF), F32),
            pltpu.VMEM((GROUP, ROWS, STATE), BF16),
            pltpu.VMEM((GROUP, ROWS, STATE), BF16),
            pltpu.VMEM((SHARDS, HEADS, HALF), F32),
            pltpu.VMEM((MIDDLE, GROUP, ROWS, STATE), BF16),
            pltpu.VMEM((ROWS, STATE), BF16),
            pltpu.VMEM((BITS, GROUP, ROWS, STATE), BF16),
            pltpu.SemaphoreType.DMA((4,)),
            pltpu.SemaphoreType.DMA((PIECES + 1,)),
            pltpu.SemaphoreType.DMA((TOKENS // HALF,)),
            pltpu.SemaphoreType.DMA((2,)),
            pltpu.SemaphoreType.DMA,
            pltpu.SemaphoreType.DMA,
            pltpu.SemaphoreType.DMA((4,)),
            pltpu.SemaphoreType.DMA((2,)),
            pltpu.SemaphoreType.DMA((2,)),
            pltpu.SemaphoreType.DMA,
            pltpu.SemaphoreType.DMA,
        ],
        compiler_params=pltpu.CompilerParams(
            collective_id=0, has_side_effects=True, vmem_limit_bytes=63 << 20
        ),
    )(mixer_input, conv_weight, log_decay, level_weight, norm_gain.reshape(1, WIDTH))
    return blocks.transpose(0, 2, 1).reshape(TOKENS, WIDTH)


def solution(mesh):
    placed = (
        P("ctx", "heads"),
        P(None, "heads"),
        P("heads", "ctx"),
        P(None, "heads", "ctx"),
        P("heads"),
    )
    return jax.shard_map(
        per_device, mesh=mesh, in_specs=placed, out_specs=P("ctx", "heads"), check_vma=False
    )
```
